768 devices in a mesh: mp: 12 (over z_lo, x), dp: 64 (over z_hi, y, core).
Axes of the slice: x: 4, y: 8, z: 12 (z_hi: 4, z_lo: 3; z = z_hi * 3 + z_lo), core: 2. Of those that a mesh axis runs over, the one named last changes fastest.
Arguments:
- hidden_pre: bfloat16 [512, 30720], P('dp', 'mp'), may hold values from -36 to 36
- grad_out: bfloat16 [512, 14848], P('dp'), may hold values from -90 to 90
- w_down: bfloat16 [30720, 14848], P('mp', 'dp'), may hold values from -0.046875 to 0.046875
Outputs:
- grad_pre: bfloat16 [512, 30720], P('dp', 'mp')
- grad_down: bfloat16 [30720, 14848], P('mp', 'dp')
The draws below stay inside these ranges and needn't reach their ends.
All inputs are finite; a program needn't handle non-finite values.
Results may differ from the reference program's by a relative error of at most 0.004.
Values may be sent and summed in bfloat16 or wider, within the bound.
A program may use at most 32 MiB of HBM per device.

```python
import jax
import jax.numpy as jnp
from jax import lax

D = 14848
FF = 30720
TOKENS = 512


def token_factor(key):
    return jax.random.normal(jax.random.fold_in(key, 5), (TOKENS, 1), jnp.float32)


def column_loading(count, lower, upper):
    index = jnp.arange(count)
    return jnp.where(index < count // 2, lower, upper).astype(jnp.float32)


def draw_hidden_pre(key, part):
    shared = token_factor(key)
    key = jax.random.fold_in(key, 11)
    key_base, key_scale = jax.random.split(key, 2)
    ramp = jnp.exp(jnp.log(3.0) * jnp.arange(FF, dtype=jnp.float32) / FF)
    spread = 0.3 * jnp.exp(jnp.log(10.0) * jax.random.uniform(key_scale, (FF,), jnp.float32))
    base = jax.random.normal(key_base, (TOKENS, FF), jnp.float32)
    loading = column_loading(FF, 0.0, 0.4)
    base = jnp.sqrt(1.0 - loading * loading) * base + loading * shared
    base = jnp.clip(base, -4.0, 4.0)
    return (base * spread * ramp).astype(jnp.bfloat16)


def draw_grad_out(key, part):
    shared = token_factor(key)
    key = jax.random.fold_in(key, 23)
    key_base, key_scale = jax.random.split(key, 2)
    spread = jnp.exp(jnp.log(10.0) * jax.random.uniform(key_scale, (D,), jnp.float32))
    ramp = jnp.exp(jnp.log(3.0) * jnp.arange(D, dtype=jnp.float32) / D)
    base = jax.random.normal(key_base, (TOKENS, D), jnp.float32)
    loading = column_loading(D, 0.0, 0.4)
    base = jnp.sqrt(1.0 - loading * loading) * base + loading * shared
    base = jnp.clip(base, -4.0, 4.0)
    return (0.25 * base * spread * ramp).astype(jnp.bfloat16)


def levels(key, extent, cuts, least, largest):
    def one(axis_at, parts):
        draws = jax.random.uniform(jax.random.fold_in(jax.random.fold_in(key, 6), axis_at), (parts,), jnp.float32, least / len(cuts), largest / len(cuts))
        return jnp.repeat(jnp.exp(draws), extent[axis_at] // parts).reshape((-1,) + (1,) * (len(extent) - axis_at - 1))

    loudness = one(*cuts[0])
    for cut in cuts[1:]:
        loudness = loudness * one(*cut)
    return loudness


def gaussian(rng, dims, scale, reach, pieces=(), kind=jnp.bfloat16):
    entries = jax.random.normal(rng, dims, jnp.float32) * scale
    if len(pieces) > 0:
        entries = levels(rng, dims, pieces, -0.22, 0.18) * entries
    return jnp.clip(entries, min=-reach, max=reach).astype(kind)


def setup_inputs(seed: int = 0) -> dict:
    arg_keys = jax.random.split(jax.random.key(seed), 4)
    hidden_pre = draw_hidden_pre(jax.random.fold_in(arg_keys[3], 71), 0)
    grad_out = draw_grad_out(jax.random.fold_in(arg_keys[3], 71), 0)
    w_down = gaussian(arg_keys[2], (FF, D), D ** -0.5, 0.046875, ((0, 12), (1, 64)))
    return dict(hidden_pre=hidden_pre, grad_out=grad_out, w_down=w_down)


root_half = 0.7071067811865476
inv_root_tau = 0.3989422804014327

def gelu_value(value):
    return 0.5 * value * (1.0 + lax.erf(value * root_half))

def gelu_slope(value):
    return 0.5 * (1.0 + lax.erf(value * root_half)) + value * jnp.exp(-0.5 * value * value) * inv_root_tau

def reference(hidden_pre, grad_out, w_down):
    dy_hidden = jnp.dot(grad_out, w_down.T, preferred_element_type=jnp.float32)
    hidden = hidden_pre.astype(jnp.float32)
    grad_pre = (dy_hidden * gelu_slope(hidden)).astype(jnp.bfloat16)
    act = gelu_value(hidden).astype(jnp.bfloat16)
    raw = jnp.dot(act.T, grad_out, preferred_element_type=jnp.float32)
    sumsq = jnp.sum(raw * raw)
    rms = jnp.sqrt(sumsq / (float(FF) * float(D)) + 1e-06)
    grad_down = (raw * jnp.minimum(1.0, 1.0 / rms)).astype(jnp.bfloat16)
    return (grad_pre, grad_down)
```

```python
import functools

import jax
import jax.numpy as jnp
from jax import lax
from jax.experimental import pallas as pl
from jax.experimental.pallas import tpu as pltpu
from jax.sharding import PartitionSpec as P

root_half = 0.7071067811865476
inv_root_tau = 0.3989422804014327

f32, bf16 = jnp.float32, jnp.bfloat16
MESH = pl.DeviceIdType.MESH

NX, NZL, NY, NZH = 4, 3, 8, 4
D, FF, TOKENS = 14848, 30720, 512
WIDE = 232
HALF = 1280
CHUNK = 256
NK = HALF // CHUNK
DZ = (0, 1, 3, 2)


def gelu_value(value):
    return 0.5 * value * (1.0 + lax.erf(value * root_half))


def gelu_slope(value):
    return (
        0.5 * (1.0 + lax.erf(value * root_half))
        + value * jnp.exp(-0.5 * value * value) * inv_root_tau
    )


def kernel(
    h_ref, g_ref, w_ref, gp_ref, gd_ref,
    slope, act_f, act_in, pf, pf_in, q, qin, gf, a_all, w_own, w_in, wp,
    dyp, sb, rb, zs, zr, fin, fin_in, raw, raw_in, gdv, ar_src, ar_in,
    local_sem, pair_s, pair_r, raw_s, raw_r, gy_s, gy_r, gz_s, gz_r, gx_s, gx_r,
    gd_s, gd_r, ay_s, ay_r, az_s, az_r, rs_s, rs_r, rz_s, rz_r, ar_s, ar_r,
):
    mp, dp = lax.axis_index("mp"), lax.axis_index("dp")
    x, zl = mp % NX, mp // NX
    c, y, zh = dp % 2, (dp // 2) % NY, dp // (2 * NY)
    oc = 1 - c

    def at(x_=None, zl_=None, c_=None, y_=None, zh_=None):
        x_ = x if x_ is None else x_
        zl_ = zl if zl_ is None else zl_
        c_ = c if c_ is None else c_
        y_ = y if y_ is None else y_
        zh_ = zh if zh_ is None else zh_
        return (zl_ * NX + x_, (zh_ * NY + y_) * 2 + c_)

    pair = at(c_=oc)
    later = []

    def copy(src, dst, ss, rs, to):
        return pltpu.make_async_remote_copy(
            src_ref=src, dst_ref=dst, send_sem=ss, recv_sem=rs, device_id=to, device_id_type=MESH
        )

    def send(src, dst, ss, rs, to):
        cp = copy(src, dst, ss, rs, to)
        cp.start()
        later.append(cp)

    def arrived(dst, ss, rs):
        copy(dst, dst, ss, rs, pair).wait_recv()

    barrier = pltpu.get_barrier_semaphore()
    peers = [pair]
    peers += [at(x_=(x + r) % NX) for r in range(1, NX)]
    peers += [at(y_=(y + r) % NY) for r in range(1, NY)]
    peers += [at(zh_=(zh + r) % NZH) for r in range(1, NZH)]
    peers += [at(zl_=(zl + r) % NZL) for r in range(1, NZL)]
    for peer in peers:
        pl.semaphore_signal(barrier, inc=1, device_id=peer, device_id_type=MESH)

    own_rows = pl.ds(pl.multiple_of(HALF * c, 16), HALF)
    other_rows = pl.ds(pl.multiple_of(HALF * oc, 16), HALF)
    w_copy = pltpu.make_async_copy(w_ref.at[own_rows], w_own, local_sem.at[0])
    w_copy.start()

    for half in range(2):
        hidden = h_ref[:, HALF * half:HALF * (half + 1)].astype(f32)
        act_f[half] = gelu_value(hidden).astype(bf16).astype(f32)
        slope[half] = gelu_slope(hidden)

    tile = x % 2
    first = WIDE * (x // 2) + 128 * tile
    lanes = lax.broadcasted_iota(jnp.int32, (8, 128), 1)
    keep = lanes < 128 - (256 - WIDE) * tile
    for d in range(NZH * NY):
        if d < NZH * NY - 1:
            off = 2 * WIDE * d + first
            start, width = (off // 128) * 128, 256
            window = g_ref[:, pl.ds(pl.multiple_of(start, 128), width)]
        else:
            off = 2 * WIDE * d + first
            start, width = D - 512, 512
            window = g_ref[:, start:start + width]
        rolled = pltpu.roll(window.astype(f32), width - (off - start), axis=1)
        pf[d] = jnp.where(keep, rolled[:, :128], 0.0)

    pl.semaphore_wait(barrier, len(peers))

    send(act_f.at[oc], act_in, pair_s.at[0], pair_r.at[0], pair)
    send(pf.at[pl.ds(16 * oc, 16)], pf_in, pair_s.at[1], pair_r.at[1], pair)
    send(w_ref.at[other_rows], w_in, pair_s.at[2], pair_r.at[2], pair)

    def rows_of(ys, zs_):
        return pl.ds(pl.multiple_of(64 * ys + 16 * zs_, 16), 16)

    def zj(j):
        return (zh + DZ[j]) % NZH

    def ys_of(way, t):
        return (y - t) % NY if way == 0 else (y + t) % NY

    def next_y(way):
        return at(y_=(y + 1) % NY) if way == 0 else at(y_=(y + NY - 1) % NY)

    def ways(t, j):
        if t < 3:
            return (0, 1)
        return (0,) if j < 2 else (1,)

    def gather(t, j):
        if t == 0 and j > 0:
            block = a_all.at[rows_of(y, zj(j))]
            arrived(block, az_s.at[j], az_r.at[j])
        for way in ways(t, j):
            block = a_all.at[rows_of(ys_of(way, t), zj(j))]
            if t > 0:
                arrived(block, ay_s.at[way, t - 1, j], ay_r.at[way, t - 1, j])
            send(block, block, ay_s.at[way, t, j], ay_r.at[way, t, j], next_y(way))

    arrived(act_in, pair_s.at[0], pair_r.at[0])
    mine, theirs = act_f[c], act_in[...]
    a_all[rows_of(y, zh), :] = jnp.concatenate(
        [jnp.where(c == 0, mine, theirs), jnp.where(c == 0, theirs, mine)], axis=0
    ).astype(bf16)
    own_block = a_all.at[rows_of(y, zh)]
    for r in (1, 3, 2):
        j = DZ.index((NZH - r) % NZH)
        send(own_block, own_block, az_s.at[j], az_r.at[j], at(zh_=(zh + r) % NZH))
    gather(0, 0)

    arrived(pf_in, pair_s.at[1], pair_r.at[1])
    for j in range(2):
        for yd in range(NY):
            mine, theirs = pf[16 * c + 8 * j + yd], pf_in[8 * j + yd]
            q[j, yd] = jnp.concatenate(
                [jnp.where(c == 0, mine, theirs), jnp.where(c == 0, theirs, mine)], axis=0
            ).astype(bf16)
    for r in range(1, NY):
        to = (y + r) % NY
        send(q.at[:, to], qin.at[:, y], gy_s.at[r], gy_r.at[r], at(y_=to))
    qin[:, pl.ds(y, 1)] = q[:, pl.ds(y, 1)]

    z16 = pl.ds(pl.multiple_of(16 * zh, 16), 16)
    holder = c == zh // 2

    def features_z():
        for r in range(1, NY):
            arrived(qin.at[:, (y + NY - r) % NY], gy_s.at[r], gy_r.at[r])
        for j in range(2):
            to = 2 * c + j

            @pl.when(to != zh)
            def _():
                copy(qin.at[j], gf.at[x, :, z16], gz_s.at[j], gz_r.at[zh], at(zh_=to)).start()

            @pl.when(to == zh)
            def _():
                gf[x, :, z16, :] = qin[j]

    def features_x():
        @pl.when(holder)
        def _():
            for r in range(1, NZH):
                src = (zh + NZH - r) % NZH
                rows = pl.ds(pl.multiple_of(16 * src, 16), 16)
                copy(gf.at[x, :, rows], gf.at[x, :, rows], gz_s.at[0], gz_r.at[src], pair).wait_recv()
            for r in range(1, NX):
                copy(gf.at[x], gf.at[x], gx_s.at[r], gx_r.at[r], at(x_=(x + r) % NX)).start()
            copy(gf.at[x], gf.at[x], gd_s.at[0], gd_r.at[0], pair).start()

    def features_pair():
        @pl.when(holder)
        def _():
            for r in range(1, NX):
                block = gf.at[(x + NX - r) % NX]
                copy(block, block, gx_s.at[r], gx_r.at[r], pair).wait_recv()
                copy(block, block, gd_s.at[r], gd_r.at[r], pair).start()

    def features_here():
        @pl.when(jnp.logical_not(holder))
        def _():
            for r in range(NX):
                block = gf.at[(x + NX - r) % NX]
                copy(block, block, gd_s.at[r], gd_r.at[r], pair).wait_recv()

    gather(1, 0)
    features_z()
    gather(0, 1)
    gather(0, 2)
    features_x()
    gather(2, 0)
    gather(1, 1)
    gather(1, 2)
    gather(0, 3)
    features_pair()
    gather(3, 0)
    gather(2, 1)
    gather(2, 2)
    gather(1, 3)
    w_copy.wait()
    arrived(w_in, pair_s.at[2], pair_r.at[2])
    wp[...] = jnp.zeros_like(wp)
    wp[:, 0:WIDE] = jnp.where(c == 0, w_own[...], w_in[...])
    wp[:, 256:256 + WIDE] = jnp.where(c == 0, w_in[...], w_own[...])
    gather(3, 1)
    gather(2, 3)
    gather(3, 2)
    features_here()
    gather(3, 3)

    def features():
        return jnp.concatenate([gf[i].reshape(TOKENS, 128) for i in range(NX)], axis=1)

    def columns(k):
        return slice(CHUNK * k, CHUNK * (k + 1))

    def partial(yd, k, low, count):
        rows = pl.ds(pl.multiple_of(64 * yd + low, 16), count)
        return dyp[rows, columns(k)]

    def reduce_step(t, k):
        for way in range(2):
            if t == 0:
                part = (slice(0, 32),)
                val = partial((y + 4) % NY, k, 32 * way, 32)
            else:
                part = ()
                yd = (y + 4 - t) % NY if way == 0 else (y + NY - 4 + t) % NY
                if t == 1:
                    inc = rb.at[way, 0, k, slice(0, 32)]
                    arrived(inc, rs_s.at[way, 0, k], rs_r.at[way, 0, k])
                    low, high = partial(yd, k, 0, 32), partial(yd, k, 32, 32)
                    if way == 0:
                        low = low + inc[...].astype(f32)
                    else:
                        high = high + inc[...].astype(f32)
                    val = jnp.concatenate([low, high], axis=0)
                else:
                    inc = rb.at[way, t - 1, k]
                    arrived(inc, rs_s.at[way, t - 1, k], rs_r.at[way, t - 1, k])
                    val = partial(yd, k, 0, 64) + inc[...].astype(f32)
            src, dst = sb.at[(way, t, k) + part], rb.at[(way, t, k) + part]
            src[...] = val.astype(bf16)
            send(src, dst, rs_s.at[way, t, k], rs_r.at[way, t, k], next_y(way))

    def reduce_z(k):
        val = partial(y, k, 0, 64)
        for way in range(2):
            inc = rb.at[way, 3, k]
            arrived(inc, rs_s.at[way, 3, k], rs_r.at[way, 3, k])
            val = val + inc[...].astype(f32)
        zs[k] = val
        for r in range(1, NZH):
            to = (zh + r) % NZH
            rows = pl.ds(pl.multiple_of(16 * to, 16), 16)
            send(zs.at[k, rows], zr.at[k, r - 1], rz_s.at[k, r - 1], rz_r.at[k, r - 1], at(zh_=to))

    def reduce_end(k):
        val = zs[k, pl.ds(pl.multiple_of(16 * zh, 16), 16), :]
        for r in range(1, NZH):
            inc = zr.at[k, r - 1]
            arrived(inc, rz_s.at[k, r - 1], rz_r.at[k, r - 1])
            val = val + inc[...]
        fin[0, :, columns(k)] = val[0:8]
        fin[1, :, columns(k)] = val[8:16]

    def product(k):
        dyp[:, columns(k)] = lax.dot_general(
            features(), wp[columns(k), :], (((1,), (1,)), ((), ())), preferred_element_type=f32
        )

    for k in range(NK):
        product(k)
        reduce_step(0, k)

    for j in range(4):
        for way in range(2):
            t = 3 if way in ways(3, j) else 2
            block = a_all.at[rows_of(ys_of(way, t + 1), zj(j))]
            arrived(block, ay_s.at[way, t, j], ay_r.at[way, t, j])

    total = jnp.zeros((8, 128), f32)
    for k in range(NK):
        reduce_step(1, k)
        val = lax.dot_general(
            a_all[:, columns(k)], features(), (((0,), (0,)), ((), ())), preferred_element_type=f32
        )
        raw[0, columns(k), :] = val[:, 0:256]
        raw[1, columns(k), :] = val[:, 256:512]
        send(raw.at[oc, columns(k)], raw_in.at[columns(k)], raw_s.at[k], raw_r.at[k], pair)
        part = jnp.sum((val * val).reshape(CHUNK // 8, 8, 512), axis=0)
        total = total + (part[:, 0:128] + part[:, 128:256] + part[:, 256:384] + part[:, 384:512])

    stages = (
        [pair],
        [at(x_=(x + r) % NX) for r in range(1, NX)],
        [at(y_=(y + r) % NY) for r in range(1, NY)],
        [at(zl_=(zl + r) % NZL) for r in range(1, NZL)],
        [at(zh_=(zh + r) % NZH) for r in range(1, NZH)],
    )
    begin = [sum(len(s) for s in stages[:i]) for i in range(len(stages) + 1)]

    def sum_send(i):
        for n, to in enumerate(stages[i]):
            slot = begin[i] + n
            send(ar_src.at[i], ar_in.at[slot], ar_s.at[slot], ar_r.at[slot], to)

    def sum_wait(i):
        val = ar_src[i]
        for slot in range(begin[i], begin[i + 1]):
            arrived(ar_in.at[slot], ar_s.at[slot], ar_r.at[slot])
            val = val + ar_in[slot]
        ar_src[i + 1] = val

    ar_src[0] = total
    sum_send(0)
    reduce_step(2, 0)
    sum_wait(0)
    sum_send(1)
    reduce_step(2, 1)
    reduce_step(2, 2)
    sum_wait(1)
    sum_send(2)
    reduce_step(2, 3)
    reduce_step(2, 4)
    sum_wait(2)
    sum_send(3)
    reduce_step(3, 0)
    reduce_step(3, 1)
    sum_wait(3)
    sum_send(4)
    reduce_step(3, 2)
    reduce_step(3, 3)
    reduce_step(3, 4)
    reduce_z(0)
    reduce_z(1)
    sum_wait(4)

    sumsq = jnp.sum(ar_src[5])
    rms = jnp.sqrt(jnp.full((8, 128), sumsq, f32) / (float(FF) * float(D)) + 1e-06)
    scale = jnp.minimum(1.0, 1.0 / rms)[0:1, 0:1]
    gdv[own_rows, :] = (raw[c] * scale)[:, :WIDE].astype(bf16)
    out0 = pltpu.make_async_copy(gdv.at[own_rows], gd_ref.at[own_rows], local_sem.at[1])
    out0.start()
    reduce_z(2)
    reduce_z(3)
    for k in range(NK):
        arrived(raw_in.at[columns(k)], raw_s.at[k], raw_r.at[k])
    gdv[other_rows, :] = (raw_in[...] * scale)[:, :WIDE].astype(bf16)
    out1 = pltpu.make_async_copy(gdv.at[other_rows], gd_ref.at[other_rows], local_sem.at[2])
    out1.start()
    reduce_z(4)

    for k in range(NK):
        reduce_end(k)
    send(fin.at[oc], fin_in, pair_s.at[3], pair_r.at[3], pair)
    mine = fin[c]
    arrived(fin_in, pair_s.at[3], pair_r.at[3])
    theirs = fin_in[...]
    gp_ref[:, 0:HALF] = (jnp.where(c == 0, mine, theirs) * slope[0]).astype(bf16)
    gp_ref[:, HALF:2 * HALF] = (jnp.where(c == 0, theirs, mine) * slope[1]).astype(bf16)

    for cp in later:
        cp.wait_send()
    for j in range(2):
        to = 2 * c + j

        @pl.when(to != zh)
        def _():
            copy(qin.at[j], gf.at[x, :, z16], gz_s.at[j], gz_r.at[zh], at(zh_=to)).wait_send()

    @pl.when(holder)
    def _():
        for r in range(1, NX):
            copy(gf.at[x], gf.at[x], gx_s.at[r], gx_r.at[r], pair).wait_send()
        for r in range(NX):
            copy(gf.at[x], gf.at[x], gd_s.at[r], gd_r.at[r], pair).wait_send()

    out0.wait()
    out1.wait()


def local(hidden_pre, grad_out, w_down):
    dma = pltpu.SemaphoreType.DMA
    vmem = pltpu.VMEM
    n_sum = 1 + (NX - 1) + (NY - 1) + (NZL - 1) + (NZH - 1)
    sems = [
        (3,), (4,), (4,), (NK,), (NK,), (NY,), (NY,), (2,), (NZH,), (NX,), (NX,),
        (NX,), (NX,), (2, 4, 4), (2, 4, 4), (4,), (4,), (2, 4, NK), (2, 4, NK),
        (NK, 3), (NK, 3), (n_sum,), (n_sum,),
    ]
    return pl.pallas_call(
        kernel,
        out_shape=(
            jax.ShapeDtypeStruct(hidden_pre.shape, bf16),
            jax.ShapeDtypeStruct(w_down.shape, bf16),
        ),
        in_specs=[
            pl.BlockSpec(memory_space=pltpu.VMEM),
            pl.BlockSpec(memory_space=pltpu.VMEM),
            pl.BlockSpec(memory_space=pl.ANY),
        ],
        out_specs=(
            pl.BlockSpec(memory_space=pltpu.VMEM),
            pl.BlockSpec(memory_space=pl.ANY),
        ),
        scratch_shapes=[
            vmem((2, 8, HALF), f32),
            vmem((2, 8, HALF), f32),
            vmem((8, HALF), f32),
            vmem((NZH * NY, 8, 128), f32),
            vmem((16, 8, 128), f32),
            vmem((2, NY, 16, 128), bf16),
            vmem((2, NY, 16, 128), bf16),
            vmem((NX, NY, 64, 128), bf16),
            vmem((TOKENS, HALF), bf16),
            vmem((HALF, WIDE), bf16),
            vmem((HALF, WIDE), bf16),
            vmem((HALF, 512), bf16),
            vmem((TOKENS, HALF), f32),
            vmem((2, 4, NK, 64, CHUNK), bf16),
            vmem((2, 4, NK, 64, CHUNK), bf16),
            vmem((NK, 64, CHUNK), f32),
            vmem((NK, 3, 16, CHUNK), f32),
            vmem((2, 8, HALF), f32),
            vmem((8, HALF), f32),
            vmem((2, HALF, 256), f32),
            vmem((HALF, 256), f32),
            vmem((2 * HALF, WIDE), bf16),
            vmem((6, 8, 128), f32),
            vmem((n_sum, 8, 128), f32),
        ] + [dma(s) for s in sems],
        compiler_params=pltpu.CompilerParams(
            collective_id=0, has_side_effects=True, vmem_limit_bytes=50 * 1024 * 1024
        ),
        cost_estimate=pl.CostEstimate(
            flops=4 * TOKENS * 2 * HALF * WIDE, bytes_accessed=6 << 20, transcendentals=0
        ),
    )(hidden_pre, grad_out, w_down)


def solution(mesh):
    placed = (P("dp", "mp"), P("dp", None), P("mp", "dp"))
    return jax.shard_map(
        local, mesh=mesh, in_specs=placed, out_specs=(P("dp", "mp"), P("mp", "dp")), check_vma=False
    )
```

```python
import functools

import jax
import jax.numpy as jnp
from jax import lax
from jax.experimental import pallas as pl
from jax.experimental.pallas import tpu as pltpu
from jax.sharding import PartitionSpec as P

root_half = 0.7071067811865476
inv_root_tau = 0.3989422804014327

f32, bf16 = jnp.float32, jnp.bfloat16
MESH = pl.DeviceIdType.MESH

NX, NZL, NY, NZH = 4, 3, 8, 4
D, FF, TOKENS = 14848, 30720, 512
WIDE = 232
HALF = 1280
CHUNK = 256
NK = HALF // CHUNK
DZ = (0, 1, 3, 2, 2)
PIECE = (slice(0, HALF),) * 3 + (slice(0, HALF // 2), slice(HALF // 2, HALF))


def gelu_value(value):
    return 0.5 * value * (1.0 + lax.erf(value * root_half))


def gelu_slope(value):
    return (
        0.5 * (1.0 + lax.erf(value * root_half))
        + value * jnp.exp(-0.5 * value * value) * inv_root_tau
    )


def kernel(
    h_ref, g_ref, w_ref, gp_ref, gd_ref,
    slope, act_f, act_in, pf, pf_in, q, qin, gf, gt, a_all, w_own, w_in, wp,
    dyp, sb, rb, zs, z1, z2, z1_in, z2_in, fin, fin_in, raw, raw_in, gdv, ar_src, ar_in,
    local_sem, pair_s, pair_r, raw_s, raw_r, gy_s, gy_r, gz_s, gz_r, gx_s, gx_r,
    gd_s, gd_r, ay_s, ay_r, az_s, az_r, rs_s, rs_r, rz_s, rz_r, fin_s, fin_r, ar_s, ar_r,
):
    mp, dp = lax.axis_index("mp"), lax.axis_index("dp")
    x, zl = mp % NX, mp // NX
    c, y, zh = dp % 2, (dp // 2) % NY, dp // (2 * NY)
    oc = 1 - c

    def at(x_=None, zl_=None, c_=None, y_=None, zh_=None):
        x_ = x if x_ is None else x_
        zl_ = zl if zl_ is None else zl_
        c_ = c if c_ is None else c_
        y_ = y if y_ is None else y_
        zh_ = zh if zh_ is None else zh_
        return (zl_ * NX + x_, (zh_ * NY + y_) * 2 + c_)

    pair = at(c_=oc)
    later = []

    def copy(src, dst, ss, rs, to):
        return pltpu.make_async_remote_copy(
            src_ref=src, dst_ref=dst, send_sem=ss, recv_sem=rs, device_id=to, device_id_type=MESH
        )

    def send(src, dst, ss, rs, to):
        cp = copy(src, dst, ss, rs, to)
        cp.start()
        later.append(cp)

    def arrived(dst, ss, rs):
        copy(dst, dst, ss, rs, pair).wait_recv()

    barrier = pltpu.get_barrier_semaphore()
    peers = [pair]
    peers += [at(x_=(x + r) % NX) for r in range(1, NX)]
    peers += [at(y_=(y + r) % NY) for r in range(1, NY)]
    depth = NZL * NZH
    along_z = [(NZL * zh + zl + r) % depth for r in range(1, depth)]
    along_z = [at(zl_=p % NZL, zh_=p // NZL) for p in along_z]
    peers += along_z
    for peer in peers:
        pl.semaphore_signal(barrier, inc=1, device_id=peer, device_id_type=MESH)

    own_cols = pl.ds(pl.multiple_of(HALF * c, 128), HALF)
    other_cols = pl.ds(pl.multiple_of(HALF * oc, 128), HALF)
    w_copy = pltpu.make_async_copy(w_ref.at[:, own_cols], w_own, local_sem.at[0])
    w_copy.start()

    tile = x % 2
    first = WIDE * (x // 2) + 128 * tile
    lanes = lax.broadcasted_iota(jnp.int32, (8, 128), 1)
    keep = lanes < 128 - (256 - WIDE) * tile
    for d in range(NZH * NY):
        if d < NZH * NY - 1:
            off = 2 * WIDE * d + first
            start, width = (off // 128) * 128, 256
            window = g_ref[:, pl.ds(pl.multiple_of(start, 128), width)]
        else:
            off = 2 * WIDE * d + first
            start, width = D - 512, 512
            window = g_ref[:, start:start + width]
        rolled = pltpu.roll(window.astype(f32), width - (off - start), axis=1)
        pf[d] = jnp.where(keep, rolled[:, :128], 0.0)

    pl.semaphore_wait(barrier, len(peers))
    send(pf.at[pl.ds(16 * oc, 16)], pf_in, pair_s.at[1], pair_r.at[1], pair)

    for half in range(2):
        hidden = h_ref[:, HALF * half:HALF * (half + 1)].astype(f32)
        act_f[half] = gelu_value(hidden).astype(bf16).astype(f32)

    send(act_f.at[oc], act_in, pair_s.at[0], pair_r.at[0], pair)

    def rows_of(ys, zs_):
        return pl.ds(pl.multiple_of(64 * ys + 16 * zs_, 16), 16)

    def zj(j):
        return (zh + DZ[j]) % NZH

    def ys_of(way, t):
        return (y - t) % NY if way == 0 else (y + t) % NY

    def next_y(way):
        return at(y_=(y + 1) % NY) if way == 0 else at(y_=(y + NY - 1) % NY)

    def ways(t, j):
        if t < 3:
            return (0, 1)
        return (0,) if j < 2 else (1,)

    def piece(ys, j):
        return a_all.at[rows_of(ys, zj(j)), PIECE[j]]

    def gather(t, j):
        if t == 0 and j > 2:
            arrived(piece(y, j), az_s.at[j], az_r.at[j])
        for way in ways(t, j):
            block = piece(ys_of(way, t), j)
            if t > 0:
                arrived(block, ay_s.at[way, t - 1, j], ay_r.at[way, t - 1, j])
            send(block, block, ay_s.at[way, t, j], ay_r.at[way, t, j], next_y(way))

    up, down = at(zh_=(zh + 1) % NZH), at(zh_=(zh + NZH - 1) % NZH)

    def relay(i):
        j, to, half = ((2, up, 3), (1, down, 4))[i]
        arrived(piece(y, j), az_s.at[j], az_r.at[j])
        block = a_all.at[rows_of(y, zj(j)), PIECE[half]]
        send(block, block, az_s.at[half], az_r.at[half], to)

    arrived(pf_in, pair_s.at[1], pair_r.at[1])
    for j in range(2):
        for yd in range(NY):
            mine, theirs = pf[16 * c + 8 * j + yd], pf_in[8 * j + yd]
            q[j, yd] = jnp.concatenate(
                [jnp.where(c == 0, mine, theirs), jnp.where(c == 0, theirs, mine)], axis=0
            ).astype(bf16)
    for r in range(1, NY):
        to = (y + r) % NY
        send(q.at[:, to], qin.at[:, y], gy_s.at[r], gy_r.at[r], at(y_=to))
    qin[:, pl.ds(y, 1)] = q[:, pl.ds(y, 1)]

    arrived(act_in, pair_s.at[0], pair_r.at[0])
    mine, theirs = act_f[c], act_in[...]
    a_all[rows_of(y, zh), :] = jnp.concatenate(
        [jnp.where(c == 0, mine, theirs), jnp.where(c == 0, theirs, mine)], axis=0
    ).astype(bf16)
    own_block = a_all.at[rows_of(y, zh)]
    send(own_block, own_block, az_s.at[2], az_r.at[2], up)
    send(own_block, own_block, az_s.at[1], az_r.at[1], down)
    gather(0, 0)

    z16 = pl.ds(pl.multiple_of(16 * zh, 16), 16)
    holder = c == zh // 2

    def token_rows(dz):
        return pl.ds(pl.multiple_of(16 * ((zh + dz) % NZH), 16), 16)

    near, far = 2 * c + 1 - zh % 2, 2 * c + zh % 2
    near_at, far_at = at(zh_=near), at(zh_=far, zl_=(zl + 1) % NZL)

    def features_z():
        for r in range(1, NY):
            arrived(qin.at[:, (y + NY - r) % NY], gy_s.at[r], gy_r.at[r])
        send(qin.at[1 - zh % 2], gf.at[x, :, z16], gz_s.at[0], gz_r.at[zh], near_at)

        @pl.when(jnp.logical_not(holder))
        def _():
            copy(qin.at[zh % 2], gf.at[x, :, z16], gz_s.at[1], gz_r.at[zh], far_at).start()

        @pl.when(holder)
        def _():
            gf[x, :, z16, :] = qin[zh % 2]

    def features_x(dz):
        @pl.when(holder)
        def _():
            block = gf.at[x, :, token_rows(dz)]
            if dz > 0:
                copy(block, block, gz_s.at[0], gz_r.at[(zh + dz) % NZH], pair).wait_recv()
            for r in range(1, NX):
                copy(block, block, gx_s.at[r, dz], gx_r.at[r, dz], at(x_=(x + r) % NX)).start()
            copy(block, block, gd_s.at[0, dz], gd_r.at[0, dz], pair).start()

    def features_pair(dz):
        @pl.when(holder)
        def _():
            for r in range(1, NX):
                block = gf.at[(x + NX - r) % NX, :, token_rows(dz)]
                copy(block, block, gx_s.at[r, dz], gx_r.at[r, dz], pair).wait_recv()
                copy(block, block, gd_s.at[r, dz], gd_r.at[r, dz], pair).start()

    def features_here():
        @pl.when(jnp.logical_not(holder))
        def _():
            for dz in range(NZH):
                for r in range(NX):
                    block = gf.at[(x + NX - r) % NX, :, token_rows(dz)]
                    copy(block, block, gd_s.at[r, dz], gd_r.at[r, dz], pair).wait_recv()

    def weights():
        w_copy.wait()
        arrived(w_in, pair_s.at[2], pair_r.at[2])
        for b in range(2):
            wp[256 * b:256 * b + WIDE, :] = jnp.where(c == b, w_own[...], w_in[...])
            wp[256 * b + WIDE:256 * (b + 1), :] = jnp.zeros((256 - WIDE, HALF), bf16)

    def features():
        return jnp.concatenate([gf[i].reshape(TOKENS, 128) for i in range(NX)], axis=1)

    def turned():
        for i in range(NX):
            gt[128 * i:128 * (i + 1), :] = gf[i].reshape(TOKENS, 128).astype(f32).T.astype(bf16)

    def columns(k):
        return slice(CHUNK * k, CHUNK * (k + 1))

    def partial(yd, k, low, count):
        rows = pl.ds(pl.multiple_of(64 * yd + low, 16), count)
        return dyp[rows, columns(k)]

    def reduce_step(t, k):
        for way in range(2):
            if t == 0:
                part = (slice(0, 32),)
                val = partial((y + 4) % NY, k, 32 * way, 32)
            else:
                part = ()
                yd = (y + 4 - t) % NY if way == 0 else (y + NY - 4 + t) % NY
                if t == 1:
                    inc = rb.at[way, 0, k, slice(0, 32)]
                    arrived(inc, rs_s.at[way, 0, k], rs_r.at[way, 0, k])
                    low, high = partial(yd, k, 0, 32), partial(yd, k, 32, 32)
                    if way == 0:
                        low = low + inc[...].astype(f32)
                    else:
                        high = high + inc[...].astype(f32)
                    val = jnp.concatenate([low, high], axis=0)
                else:
                    inc = rb.at[way, t - 1, k]
                    arrived(inc, rs_s.at[way, t - 1, k], rs_r.at[way, t - 1, k])
                    val = partial(yd, k, 0, 64) + inc[...].astype(f32)
            src, dst = sb.at[(way, t, k) + part], rb.at[(way, t, k) + part]
            src[...] = val.astype(bf16)
            send(src, dst, rs_s.at[way, t, k], rs_r.at[way, t, k], next_y(way))

    def z_rows(dz):
        return pl.ds(pl.multiple_of(16 * ((zh + dz) % NZH), 16), 16)

    def reduce_z(k):
        val = partial(y, k, 0, 64)
        for way in range(2):
            inc = rb.at[way, 3, k]
            arrived(inc, rs_s.at[way, 3, k], rs_r.at[way, 3, k])
            val = val + inc[...].astype(f32)
        zs[k] = val
        for way, to in ((0, up), (1, down)):
            z1[k, way] = zs[k, z_rows(2), 128 * way:128 * (way + 1)]
            send(z1.at[k, way], z1_in.at[k, way], rz_s.at[k, way], rz_r.at[k, way], to)

    def reduce_z2(k):
        for way, to in ((0, up), (1, down)):
            arrived(z1_in.at[k, way], rz_s.at[k, way], rz_r.at[k, way])
            val = zs[k, z_rows(1 if way == 0 else 3), :]
            inc = z1_in[k, way]
            parts = [val[:, :128], val[:, 128:]]
            parts[way] = parts[way] + inc
            z2[k, way] = jnp.concatenate(parts, axis=1)
            send(z2.at[k, way], z2_in.at[k, way], rz_s.at[k, 2 + way], rz_r.at[k, 2 + way], to)

    def reduce_end(k):
        val = zs[k, z_rows(0), :]
        for way in range(2):
            arrived(z2_in.at[k, way], rz_s.at[k, 2 + way], rz_r.at[k, 2 + way])
            val = val + z2_in[k, way]
        fin[k, 0] = val[0:8]
        fin[k, 1] = val[8:16]
        send(fin.at[k, oc], fin_in.at[k], fin_s.at[k], fin_r.at[k], pair)

    def product(k):
        dyp[:, columns(k)] = lax.dot_general(
            features(), wp[:, columns(k)], (((1,), (0,)), ((), ())), preferred_element_type=f32
        )

    def gathered():
        for j in range(len(DZ)):
            for way in range(2):
                t = 3 if way in ways(3, j) else 2
                arrived(piece(ys_of(way, t + 1), j), ay_s.at[way, t, j], ay_r.at[way, t, j])

    def weight_grad(k):
        val = lax.dot_general(
            gt[...], a_all[:, columns(k)], (((1,), (0,)), ((), ())), preferred_element_type=f32
        )
        for b in range(2):
            raw[b, :, columns(k)] = val[256 * b:256 * b + WIDE]
        send(
            raw.at[oc, :, columns(k)], raw_in.at[:, columns(k)], raw_s.at[k], raw_r.at[k], pair
        )
        part = jnp.sum((val * val).reshape(512 // 8, 8, CHUNK), axis=0)
        part = part[:, 0:128] + part[:, 128:256]
        ar_src[0] = part if k == 0 else ar_src[0] + part

    stages = (
        [pair],
        [at(x_=(x + r) % NX) for r in range(1, NX)],
        [at(y_=(y + r) % NY) for r in range(1, NY)],
        along_z,
    )
    begin = [sum(len(s) for s in stages[:i]) for i in range(len(stages) + 1)]

    def sum_send(i):
        for n, to in enumerate(stages[i]):
            slot = begin[i] + n
            send(ar_src.at[i], ar_in.at[slot], ar_s.at[slot], ar_r.at[slot], to)

    def sum_wait(i):
        val = ar_src[i]
        for slot in range(begin[i], begin[i + 1]):
            arrived(ar_in.at[slot], ar_s.at[slot], ar_r.at[slot])
            val = val + ar_in[slot]
        ar_src[i + 1] = val

    def scaled():
        sumsq = jnp.sum(ar_src[4])
        rms = jnp.sqrt(jnp.full((8, 128), sumsq, f32) / (float(FF) * float(D)) + 1e-06)
        scale = jnp.minimum(1.0, 1.0 / rms)[0:1, 0:1]
        gdv[:, own_cols] = (raw[c] * scale).astype(bf16)
        out0 = pltpu.make_async_copy(gdv.at[:, own_cols], gd_ref.at[:, own_cols], local_sem.at[1])
        out0.start()
        for k in range(NK):
            arrived(raw_in.at[:, columns(k)], raw_s.at[k], raw_r.at[k])
        gdv[:, other_cols] = (raw_in[...] * scale).astype(bf16)
        out1 = pltpu.make_async_copy(
            gdv.at[:, other_cols], gd_ref.at[:, other_cols], local_sem.at[2]
        )
        out1.start()
        return out0, out1

    def slopes():
        for half in range(2):
            slope[half] = gelu_slope(h_ref[:, HALF * half:HALF * (half + 1)].astype(f32))

    send(w_ref.at[:, other_cols], w_in, pair_s.at[2], pair_r.at[2], pair)
    slopes()
    weights()
    gather(1, 0)
    features_z()
    features_x(0)
    relay(0)
    relay(1)
    gather(0, 2)
    gather(0, 1)
    gather(2, 0)
    gather(1, 2)
    features_pair(0)
    features_x(1)
    features_x(3)
    gather(1, 1)
    gather(3, 0)
    gather(0, 3)
    features_x(2)
    gather(0, 4)
    gather(2, 2)
    gather(2, 1)
    features_pair(1)
    gather(1, 3)
    features_pair(3)
    gather(1, 4)
    features_pair(2)
    gather(3, 2)
    gather(3, 1)
    features_here()
    gather(2, 3)
    turned()
    gather(2, 4)
    product(0)
    reduce_step(0, 0)
    product(1)
    reduce_step(0, 1)
    product(2)
    reduce_step(0, 2)
    product(3)
    reduce_step(0, 3)
    product(4)
    reduce_step(0, 4)
    gather(3, 3)
    gather(3, 4)
    reduce_step(1, 0)
    reduce_step(1, 1)
    reduce_step(1, 2)
    reduce_step(1, 3)
    reduce_step(1, 4)
    gathered()
    weight_grad(0)
    weight_grad(1)
    reduce_step(2, 0)
    weight_grad(2)
    weight_grad(3)
    weight_grad(4)
    sum_send(0)
    reduce_step(2, 1)
    reduce_step(2, 2)
    sum_wait(0)
    sum_send(1)
    reduce_step(2, 3)
    reduce_step(2, 4)
    reduce_step(3, 0)
    reduce_step(3, 1)
    sum_wait(1)
    sum_send(2)
    reduce_step(3, 2)
    reduce_step(3, 3)
    reduce_step(3, 4)
    reduce_z(0)
    reduce_z(1)
    reduce_z(2)
    sum_wait(2)
    sum_send(3)
    reduce_z(3)
    reduce_z(4)
    reduce_z2(0)
    reduce_z2(1)
    reduce_z2(2)
    reduce_z2(3)
    reduce_z2(4)
    sum_wait(3)
    reduce_end(0)
    outs = scaled()
    reduce_end(1)
    reduce_end(2)
    reduce_end(3)
    reduce_end(4)

    for k in range(NK):
        arrived(fin_in.at[k], fin_s.at[k], fin_r.at[k])
        mine, theirs = fin[k, c], fin_in[k]
        for half in range(2):
            cols = slice(HALF * half + CHUNK * k, HALF * half + CHUNK * (k + 1))
            gp_ref[:, cols] = (jnp.where(c == half, mine, theirs) * slope[half, :, columns(k)]).astype(bf16)

    for cp in later:
        cp.wait_send()
    @pl.when(jnp.logical_not(holder))
    def _():
        copy(qin.at[0], gf.at[x, :, z16], gz_s.at[1], gz_r.at[zh], pair).wait_send()

    @pl.when(holder)
    def _():
        for dz in range(NZH):
            block = gf.at[x, :, token_rows(dz)]
            for r in range(NX):
                if r > 0:
                    copy(block, block, gx_s.at[r, dz], gx_r.at[r, dz], pair).wait_send()
                copy(block, block, gd_s.at[r, dz], gd_r.at[r, dz], pair).wait_send()

    for out in outs:
        out.wait()


def local(hidden_pre, grad_out, w_down):
    dma = pltpu.SemaphoreType.DMA
    vmem = pltpu.VMEM
    n_sum = 1 + (NX - 1) + (NY - 1) + (NZL * NZH - 1)
    sems = [
        (3,), (3,), (3,), (NK,), (NK,), (NY,), (NY,), (2,), (NZH,), (NX, NZH), (NX, NZH),
        (NX, NZH), (NX, NZH), (2, 4, 5), (2, 4, 5), (5,), (5,), (2, 4, NK), (2, 4, NK),
        (NK, 4), (NK, 4), (NK,), (NK,), (n_sum,), (n_sum,),
    ]
    grad_pre, grad_down = pl.pallas_call(
        kernel,
        out_shape=(
            jax.ShapeDtypeStruct(hidden_pre.shape, bf16),
            jax.ShapeDtypeStruct(w_down.T.shape, bf16),
        ),
        in_specs=[
            pl.BlockSpec(memory_space=pltpu.VMEM),
            pl.BlockSpec(memory_space=pltpu.VMEM),
            pl.BlockSpec(memory_space=pl.ANY),
        ],
        out_specs=(
            pl.BlockSpec(memory_space=pltpu.VMEM),
            pl.BlockSpec(memory_space=pl.ANY),
        ),
        scratch_shapes=[
            vmem((2, 8, HALF), f32),
            vmem((2, 8, HALF), f32),
            vmem((8, HALF), f32),
            vmem((NZH * NY, 8, 128), f32),
            vmem((16, 8, 128), f32),
            vmem((2, NY, 16, 128), bf16),
            vmem((2, NY, 16, 128), bf16),
            vmem((NX, NY, 64, 128), bf16),
            vmem((512, TOKENS), bf16),
            vmem((TOKENS, HALF), bf16),
            vmem((WIDE, HALF), bf16),
            vmem((WIDE, HALF), bf16),
            vmem((512, HALF), bf16),
            vmem((TOKENS, HALF), f32),
            vmem((2, 4, NK, 64, CHUNK), bf16),
            vmem((2, 4, NK, 64, CHUNK), bf16),
            vmem((NK, 64, CHUNK), f32),
            vmem((NK, 2, 16, 128), f32),
            vmem((NK, 2, 16, CHUNK), f32),
            vmem((NK, 2, 16, 128), f32),
            vmem((NK, 2, 16, CHUNK), f32),
            vmem((NK, 2, 8, CHUNK), f32),
            vmem((NK, 8, CHUNK), f32),
            vmem((2, WIDE, HALF), f32),
            vmem((WIDE, HALF), f32),
            vmem((WIDE, 2 * HALF), bf16),
            vmem((5, 8, 128), f32),
            vmem((n_sum, 8, 128), f32),
        ] + [dma(s) for s in sems],
        compiler_params=pltpu.CompilerParams(
            collective_id=0, has_side_effects=True, vmem_limit_bytes=50 * 1024 * 1024
        ),
        cost_estimate=pl.CostEstimate(
            flops=4 * TOKENS * 2 * HALF * WIDE, bytes_accessed=6 << 20, transcendentals=0
        ),
    )(hidden_pre, grad_out, w_down.T)
    return grad_pre, grad_down.T


def solution(mesh):
    placed = (P("dp", "mp"), P("dp", None), P("mp", "dp"))
    return jax.shard_map(
        local, mesh=mesh, in_specs=placed, out_specs=(P("dp", "mp"), P("mp", "dp")), check_vma=False
    )
```

```python
import functools

import jax
import jax.numpy as jnp
from jax import lax
from jax.experimental import pallas as pl
from jax.experimental.pallas import tpu as pltpu
from jax.sharding import PartitionSpec as P

root_half = 0.7071067811865476
inv_root_tau = 0.3989422804014327

f32, bf16 = jnp.float32, jnp.bfloat16
MESH = pl.DeviceIdType.MESH

NX, NZL, NY, NZH = 4, 3, 8, 4
D, FF, TOKENS = 14848, 30720, 512
WIDE = 232
HALF = 1280
CHUNK = 256
NK = HALF // CHUNK
DZ = (0, 1, 3, 2, 2)
PIECE = (slice(0, HALF),) * 3 + (slice(0, HALF // 2), slice(HALF // 2, HALF))


def gelu_value(value):
    return 0.5 * value * (1.0 + lax.erf(value * root_half))


def gelu_slope(value):
    return (
        0.5 * (1.0 + lax.erf(value * root_half))
        + value * jnp.exp(-0.5 * value * value) * inv_root_tau
    )


def kernel(
    h_hbm, g_hbm, w_ref, gp_ref, gd_ref,
    h_ref, g_ref, slope, act_f, act_in, pf, pf_in, q, qin, gf, gt, a_all, w_own, w_in, wp,
    dyp, sb, rb, zs, z1, z2, z1_in, z2_in, fin, fin_in, raw, raw_in, gdv, ar_src, ar_in,
    local_sem, pair_s, pair_r, raw_s, raw_r, gy_s, gy_r, gz_s, gz_r, gx_s, gx_r,
    gd_s, gd_r, ay_s, ay_r, az_s, az_r, rs_s, rs_r, rz_s, rz_r, fin_s, fin_r, ar_s, ar_r,
):
    mp, dp = lax.axis_index("mp"), lax.axis_index("dp")
    x, zl = mp % NX, mp // NX
    c, y, zh = dp % 2, (dp // 2) % NY, dp // (2 * NY)
    oc = 1 - c

    def at(x_=None, zl_=None, c_=None, y_=None, zh_=None):
        x_ = x if x_ is None else x_
        zl_ = zl if zl_ is None else zl_
        c_ = c if c_ is None else c_
        y_ = y if y_ is None else y_
        zh_ = zh if zh_ is None else zh_
        return (zl_ * NX + x_, (zh_ * NY + y_) * 2 + c_)

    pair = at(c_=oc)
    later = []

    def copy(src, dst, ss, rs, to):
        return pltpu.make_async_remote_copy(
            src_ref=src, dst_ref=dst, send_sem=ss, recv_sem=rs, device_id=to, device_id_type=MESH
        )

    def send(src, dst, ss, rs, to):
        cp = copy(src, dst, ss, rs, to)
        cp.start()
        later.append(cp)

    def arrived(dst, ss, rs):
        copy(dst, dst, ss, rs, pair).wait_recv()

    g_copy = pltpu.make_async_copy(g_hbm, g_ref, local_sem.at[3])
    h_copy = pltpu.make_async_copy(h_hbm, h_ref, local_sem.at[4])
    g_copy.start()
    h_copy.start()
    barrier = pltpu.get_barrier_semaphore()
    depth = NZL * NZH
    along_z = [(NZL * zh + zl + r) % depth for r in range(1, depth)]
    along_z = [at(zl_=p % NZL, zh_=p // NZL) for p in along_z]
    along_y = [at(y_=(y + r) % NY) for r in range(1, NY)]
    along_x = [at(x_=(x + r) % NX) for r in range(1, NX)]
    peers = [along_z[r - 1] for r in (6, 5, 7, 4, 8, 3, 9)]
    peers += [along_y[r - 1] for r in (4, 3, 5, 2, 6)]
    peers += [along_z[r - 1] for r in (2, 10)] + [along_x[1]]
    peers += [along_y[0], along_y[6], along_x[0], along_x[2], along_z[0], along_z[10], pair]
    for peer in peers:
        pl.semaphore_signal(barrier, inc=1, device_id=peer, device_id_type=MESH)

    own_cols = pl.ds(pl.multiple_of(HALF * c, 128), HALF)
    other_cols = pl.ds(pl.multiple_of(HALF * oc, 128), HALF)
    w_copy = pltpu.make_async_copy(w_ref.at[:, own_cols], w_own, local_sem.at[0])
    w_copy.start()

    g_copy.wait()

    tile = x % 2
    first = WIDE * (x // 2) + 128 * tile
    lanes = lax.broadcasted_iota(jnp.int32, (8, 128), 1)
    keep = lanes < 128 - (256 - WIDE) * tile
    for d in range(NZH * NY):
        if d < NZH * NY - 1:
            off = 2 * WIDE * d + first
            start, width = (off // 128) * 128, 256
            window = g_ref[:, pl.ds(pl.multiple_of(start, 128), width)]
        else:
            off = 2 * WIDE * d + first
            start, width = D - 512, 512
            window = g_ref[:, start:start + width]
        rolled = pltpu.roll(window.astype(f32), width - (off - start), axis=1)
        pf[d] = jnp.where(keep, rolled[:, :128], 0.0)

    h_copy.wait()
    for half in range(2):
        hidden = h_ref[:, HALF * half:HALF * (half + 1)].astype(f32)
        act_f[half] = gelu_value(hidden).astype(bf16).astype(f32)

    pl.semaphore_wait(barrier, len(peers))
    send(pf.at[pl.ds(16 * oc, 16)], pf_in, pair_s.at[1], pair_r.at[1], pair)
    send(act_f.at[oc], act_in, pair_s.at[0], pair_r.at[0], pair)

    def rows_of(ys, zs_):
        return pl.ds(pl.multiple_of(64 * ys + 16 * zs_, 16), 16)

    def zj(j):
        return (zh + DZ[j]) % NZH

    def ys_of(way, t):
        return (y - t) % NY if way == 0 else (y + t) % NY

    def next_y(way):
        return at(y_=(y + 1) % NY) if way == 0 else at(y_=(y + NY - 1) % NY)

    def ways(t, j):
        if t < 3:
            return (0, 1)
        return (0,) if j < 2 else (1,)

    def piece(ys, j):
        return a_all.at[rows_of(ys, zj(j)), PIECE[j]]

    def gather(t, j):
        if t == 0 and j > 2:
            arrived(piece(y, j), az_s.at[j], az_r.at[j])
        for way in ways(t, j):
            block = piece(ys_of(way, t), j)
            if t > 0:
                arrived(block, ay_s.at[way, t - 1, j], ay_r.at[way, t - 1, j])
            send(block, block, ay_s.at[way, t, j], ay_r.at[way, t, j], next_y(way))

    up, down = at(zh_=(zh + 1) % NZH), at(zh_=(zh + NZH - 1) % NZH)

    def relay(i):
        j, to, half = ((2, up, 3), (1, down, 4))[i]
        arrived(piece(y, j), az_s.at[j], az_r.at[j])
        block = a_all.at[rows_of(y, zj(j)), PIECE[half]]
        send(block, block, az_s.at[half], az_r.at[half], to)

    arrived(pf_in, pair_s.at[1], pair_r.at[1])
    for j in range(2):
        for yd in range(NY):
            mine, theirs = pf[16 * c + 8 * j + yd], pf_in[8 * j + yd]
            q[j, yd] = jnp.concatenate(
                [jnp.where(c == 0, mine, theirs), jnp.where(c == 0, theirs, mine)], axis=0
            ).astype(bf16)
    for r in range(1, NY):
        to = (y + r) % NY
        send(q.at[:, to], qin.at[:, y], gy_s.at[r], gy_r.at[r], at(y_=to))
    qin[:, pl.ds(y, 1)] = q[:, pl.ds(y, 1)]

    arrived(act_in, pair_s.at[0], pair_r.at[0])
    mine, theirs = act_f[c], act_in[...]
    a_all[rows_of(y, zh), :] = jnp.concatenate(
        [jnp.where(c == 0, mine, theirs), jnp.where(c == 0, theirs, mine)], axis=0
    ).astype(bf16)
    own_block = a_all.at[rows_of(y, zh)]
    send(own_block, own_block, az_s.at[2], az_r.at[2], up)
    send(own_block, own_block, az_s.at[1], az_r.at[1], down)
    gather(0, 0)

    z16 = pl.ds(pl.multiple_of(16 * zh, 16), 16)
    holder = c == zh // 2

    def token_rows(dz):
        return pl.ds(pl.multiple_of(16 * ((zh + dz) % NZH), 16), 16)

    near, far = 2 * c + 1 - zh % 2, 2 * c + zh % 2
    near_at, far_at = at(zh_=near), at(zh_=far, zl_=(zl + 1) % NZL)

    def features_z():
        for r in range(1, NY):
            arrived(qin.at[:, (y + NY - r) % NY], gy_s.at[r], gy_r.at[r])
        send(qin.at[1 - zh % 2], gf.at[x, :, z16], gz_s.at[0], gz_r.at[zh], near_at)

        @pl.when(jnp.logical_not(holder))
        def _():
            copy(qin.at[zh % 2], gf.at[x, :, z16], gz_s.at[1], gz_r.at[zh], far_at).start()

        @pl.when(holder)
        def _():
            gf[x, :, z16, :] = qin[zh % 2]

    def features_x(dz):
        @pl.when(holder)
        def _():
            block = gf.at[x, :, token_rows(dz)]
            if dz > 0:
                copy(block, block, gz_s.at[0], gz_r.at[(zh + dz) % NZH], pair).wait_recv()
            for r in range(1, NX):
                copy(block, block, gx_s.at[r, dz], gx_r.at[r, dz], at(x_=(x + r) % NX)).start()
            copy(block, block, gd_s.at[0, dz], gd_r.at[0, dz], pair).start()

    def features_pair(dz):
        @pl.when(holder)
        def _():
            for r in range(1, NX):
                block = gf.at[(x + NX - r) % NX, :, token_rows(dz)]
                copy(block, block, gx_s.at[r, dz], gx_r.at[r, dz], pair).wait_recv()
                copy(block, block, gd_s.at[r, dz], gd_r.at[r, dz], pair).start()

    def features_here():
        @pl.when(jnp.logical_not(holder))
        def _():
            for dz in range(NZH):
                for r in range(NX):
                    block = gf.at[(x + NX - r) % NX, :, token_rows(dz)]
                    copy(block, block, gd_s.at[r, dz], gd_r.at[r, dz], pair).wait_recv()

    def weights():
        w_copy.wait()
        arrived(w_in, pair_s.at[2], pair_r.at[2])
        for b in range(2):
            wp[256 * b:256 * b + WIDE, :] = jnp.where(c == b, w_own[...], w_in[...])
            wp[256 * b + WIDE:256 * (b + 1), :] = jnp.zeros((256 - WIDE, HALF), bf16)

    def features():
        return jnp.concatenate([gf[i].reshape(TOKENS, 128) for i in range(NX)], axis=1)

    def turned():
        for i in range(NX):
            gt[128 * i:128 * (i + 1), :] = gf[i].reshape(TOKENS, 128).astype(f32).T.astype(bf16)

    def columns(k):
        return slice(CHUNK * k, CHUNK * (k + 1))

    def partial(yd, k, low, count):
        rows = pl.ds(pl.multiple_of(64 * yd + low, 16), count)
        return dyp[rows, columns(k)]

    def reduce_step(t, k):
        for way in range(2):
            if t == 0:
                part = (slice(0, 32),)
                val = partial((y + 4) % NY, k, 32 * way, 32)
            else:
                part = ()
                yd = (y + 4 - t) % NY if way == 0 else (y + NY - 4 + t) % NY
                if t == 1:
                    inc = rb.at[way, 0, k, slice(0, 32)]
                    arrived(inc, rs_s.at[way, 0, k], rs_r.at[way, 0, k])
                    low, high = partial(yd, k, 0, 32), partial(yd, k, 32, 32)
                    if way == 0:
                        low = low + inc[...].astype(f32)
                    else:
                        high = high + inc[...].astype(f32)
                    val = jnp.concatenate([low, high], axis=0)
                else:
                    inc = rb.at[way, t - 1, k]
                    arrived(inc, rs_s.at[way, t - 1, k], rs_r.at[way, t - 1, k])
                    val = partial(yd, k, 0, 64) + inc[...].astype(f32)
            src, dst = sb.at[(way, t, k) + part], rb.at[(way, t, k) + part]
            src[...] = val.astype(bf16)
            send(src, dst, rs_s.at[way, t, k], rs_r.at[way, t, k], next_y(way))

    def z_rows(dz):
        return pl.ds(pl.multiple_of(16 * ((zh + dz) % NZH), 16), 16)

    def reduce_z(k):
        val = partial(y, k, 0, 64)
        for way in range(2):
            inc = rb.at[way, 3, k]
            arrived(inc, rs_s.at[way, 3, k], rs_r.at[way, 3, k])
            val = val + inc[...].astype(f32)
        zs[k] = val
        for way, to in ((0, up), (1, down)):
            z1[k, way] = zs[k, z_rows(2), 128 * way:128 * (way + 1)]
            send(z1.at[k, way], z1_in.at[k, way], rz_s.at[k, way], rz_r.at[k, way], to)

    def reduce_z2(k):
        for way, to in ((0, up), (1, down)):
            arrived(z1_in.at[k, way], rz_s.at[k, way], rz_r.at[k, way])
            val = zs[k, z_rows(1 if way == 0 else 3), :]
            inc = z1_in[k, way]
            parts = [val[:, :128], val[:, 128:]]
            parts[way] = parts[way] + inc
            z2[k, way] = jnp.concatenate(parts, axis=1)
            send(z2.at[k, way], z2_in.at[k, way], rz_s.at[k, 2 + way], rz_r.at[k, 2 + way], to)

    def reduce_end(k):
        val = zs[k, z_rows(0), :]
        for way in range(2):
            arrived(z2_in.at[k, way], rz_s.at[k, 2 + way], rz_r.at[k, 2 + way])
            val = val + z2_in[k, way]
        fin[k, 0] = val[0:8]
        fin[k, 1] = val[8:16]
        send(fin.at[k, oc], fin_in.at[k], fin_s.at[k], fin_r.at[k], pair)

    def product(k):
        dyp[:, columns(k)] = lax.dot_general(
            features(), wp[:, columns(k)], (((1,), (0,)), ((), ())), preferred_element_type=f32
        )

    def gathered():
        for j in range(len(DZ)):
            for way in range(2):
                t = 3 if way in ways(3, j) else 2
                arrived(piece(ys_of(way, t + 1), j), ay_s.at[way, t, j], ay_r.at[way, t, j])

    def weight_grad(k):
        val = lax.dot_general(
            gt[...], a_all[:, columns(k)], (((1,), (0,)), ((), ())), preferred_element_type=f32
        )
        for b in range(2):
            raw[b, :, columns(k)] = val[256 * b:256 * b + WIDE]
        send(
            raw.at[oc, :, columns(k)], raw_in.at[:, columns(k)], raw_s.at[k], raw_r.at[k], pair
        )
        part = jnp.sum((val * val).reshape(512 // 8, 8, CHUNK), axis=0)
        part = part[:, 0:128] + part[:, 128:256]
        ar_src[0] = part if k == 0 else ar_src[0] + part

    stages = (
        [pair],
        [at(x_=(x + r) % NX) for r in range(1, NX)],
        [at(y_=(y + r) % NY) for r in range(1, NY)],
        along_z,
    )
    begin = [sum(len(s) for s in stages[:i]) for i in range(len(stages) + 1)]

    def sum_send(i):
        for n, to in enumerate(stages[i]):
            slot = begin[i] + n
            send(ar_src.at[i], ar_in.at[slot], ar_s.at[slot], ar_r.at[slot], to)

    def sum_wait(i):
        val = ar_src[i]
        for slot in range(begin[i], begin[i + 1]):
            arrived(ar_in.at[slot], ar_s.at[slot], ar_r.at[slot])
            val = val + ar_in[slot]
        ar_src[i + 1] = val

    def scaled():
        sumsq = jnp.sum(ar_src[4])
        rms = jnp.sqrt(jnp.full((8, 128), sumsq, f32) / (float(FF) * float(D)) + 1e-06)
        scale = jnp.minimum(1.0, 1.0 / rms)[0:1, 0:1]
        gdv[:, own_cols] = (raw[c] * scale).astype(bf16)
        out0 = pltpu.make_async_copy(gdv.at[:, own_cols], gd_ref.at[:, own_cols], local_sem.at[1])
        out0.start()
        for k in range(NK):
            arrived(raw_in.at[:, columns(k)], raw_s.at[k], raw_r.at[k])
        gdv[:, other_cols] = (raw_in[...] * scale).astype(bf16)
        out1 = pltpu.make_async_copy(
            gdv.at[:, other_cols], gd_ref.at[:, other_cols], local_sem.at[2]
        )
        out1.start()
        return out0, out1

    def slopes():
        for half in range(2):
            slope[half] = gelu_slope(h_ref[:, HALF * half:HALF * (half + 1)].astype(f32))

    send(w_ref.at[:, other_cols], w_in, pair_s.at[2], pair_r.at[2], pair)
    slopes()
    weights()
    gather(1, 0)
    features_z()
    features_x(0)
    relay(0)
    relay(1)
    gather(0, 2)
    gather(0, 1)
    gather(2, 0)
    gather(1, 2)
    features_pair(0)
    features_x(1)
    features_x(3)
    gather(1, 1)
    gather(3, 0)
    gather(0, 3)
    features_x(2)
    gather(0, 4)
    gather(2, 2)
    gather(2, 1)
    features_pair(1)
    gather(1, 3)
    features_pair(3)
    gather(1, 4)
    features_pair(2)
    gather(3, 2)
    gather(3, 1)
    features_here()
    gather(2, 3)
    gather(2, 4)
    product(0)
    reduce_step(0, 0)
    product(1)
    reduce_step(0, 1)
    product(2)
    reduce_step(0, 2)
    product(3)
    reduce_step(0, 3)
    product(4)
    reduce_step(0, 4)
    gather(3, 3)
    gather(3, 4)
    reduce_step(1, 0)
    reduce_step(1, 1)
    reduce_step(1, 2)
    reduce_step(1, 3)
    reduce_step(1, 4)
    turned()
    gathered()
    weight_grad(0)
    weight_grad(1)
    reduce_step(2, 0)
    weight_grad(2)
    weight_grad(3)
    weight_grad(4)
    sum_send(0)
    reduce_step(2, 1)
    reduce_step(2, 2)
    reduce_step(2, 3)
    reduce_step(2, 4)
    sum_wait(0)
    sum_send(1)
    reduce_step(3, 0)
    reduce_step(3, 1)
    reduce_step(3, 2)
    sum_wait(1)
    sum_send(2)
    reduce_step(3, 3)
    reduce_step(3, 4)
    reduce_z(0)
    reduce_z(1)
    reduce_z(2)
    reduce_z(3)
    reduce_z(4)
    reduce_z2(0)
    reduce_z2(1)
    sum_wait(2)
    sum_send(3)
    reduce_z2(2)
    reduce_z2(3)
    reduce_z2(4)
    reduce_end(0)
    reduce_end(1)
    reduce_end(2)
    reduce_end(3)
    reduce_end(4)
    sum_wait(3)
    outs = scaled()

    for k in range(NK):
        arrived(fin_in.at[k], fin_s.at[k], fin_r.at[k])
        mine, theirs = fin[k, c], fin_in[k]
        for half in range(2):
            cols = slice(HALF * half + CHUNK * k, HALF * half + CHUNK * (k + 1))
            gp_ref[:, cols] = (jnp.where(c == half, mine, theirs) * slope[half, :, columns(k)]).astype(bf16)

    for cp in later:
        cp.wait_send()
    @pl.when(jnp.logical_not(holder))
    def _():
        copy(qin.at[0], gf.at[x, :, z16], gz_s.at[1], gz_r.at[zh], pair).wait_send()

    @pl.when(holder)
    def _():
        for dz in range(NZH):
            block = gf.at[x, :, token_rows(dz)]
            for r in range(NX):
                if r > 0:
                    copy(block, block, gx_s.at[r, dz], gx_r.at[r, dz], pair).wait_send()
                copy(block, block, gd_s.at[r, dz], gd_r.at[r, dz], pair).wait_send()

    for out in outs:
        out.wait()


def local(hidden_pre, grad_out, w_down):
    dma = pltpu.SemaphoreType.DMA
    vmem = pltpu.VMEM
    n_sum = 1 + (NX - 1) + (NY - 1) + (NZL * NZH - 1)
    sems = [
        (5,), (3,), (3,), (NK,), (NK,), (NY,), (NY,), (2,), (NZH,), (NX, NZH), (NX, NZH),
        (NX, NZH), (NX, NZH), (2, 4, 5), (2, 4, 5), (5,), (5,), (2, 4, NK), (2, 4, NK),
        (NK, 4), (NK, 4), (NK,), (NK,), (n_sum,), (n_sum,),
    ]
    grad_pre, grad_down = pl.pallas_call(
        kernel,
        out_shape=(
            jax.ShapeDtypeStruct(hidden_pre.shape, bf16),
            jax.ShapeDtypeStruct(w_down.T.shape, bf16),
        ),
        in_specs=[
            pl.BlockSpec(memory_space=pl.ANY),
            pl.BlockSpec(memory_space=pl.ANY),
            pl.BlockSpec(memory_space=pl.ANY),
        ],
        out_specs=(
            pl.BlockSpec(memory_space=pltpu.VMEM),
            pl.BlockSpec(memory_space=pl.ANY),
        ),
        scratch_shapes=[
            vmem((8, 2 * HALF), bf16),
            vmem((8, D), bf16),
            vmem((2, 8, HALF), f32),
            vmem((2, 8, HALF), f32),
            vmem((8, HALF), f32),
            vmem((NZH * NY, 8, 128), f32),
            vmem((16, 8, 128), f32),
            vmem((2, NY, 16, 128), bf16),
            vmem((2, NY, 16, 128), bf16),
            vmem((NX, NY, 64, 128), bf16),
            vmem((512, TOKENS), bf16),
            vmem((TOKENS, HALF), bf16),
            vmem((WIDE, HALF), bf16),
            vmem((WIDE, HALF), bf16),
            vmem((512, HALF), bf16),
            vmem((TOKENS, HALF), f32),
            vmem((2, 4, NK, 64, CHUNK), bf16),
            vmem((2, 4, NK, 64, CHUNK), bf16),
            vmem((NK, 64, CHUNK), f32),
            vmem((NK, 2, 16, 128), f32),
            vmem((NK, 2, 16, CHUNK), f32),
            vmem((NK, 2, 16, 128), f32),
            vmem((NK, 2, 16, CHUNK), f32),
            vmem((NK, 2, 8, CHUNK), f32),
            vmem((NK, 8, CHUNK), f32),
            vmem((2, WIDE, HALF), f32),
            vmem((WIDE, HALF), f32),
            vmem((WIDE, 2 * HALF), bf16),
            vmem((5, 8, 128), f32),
            vmem((n_sum, 8, 128), f32),
        ] + [dma(s) for s in sems],
        compiler_params=pltpu.CompilerParams(
            collective_id=0, has_side_effects=True, vmem_limit_bytes=63 * 1024 * 1024
        ),
        cost_estimate=pl.CostEstimate(
            flops=4 * TOKENS * 2 * HALF * WIDE, bytes_accessed=6 << 20, transcendentals=0
        ),
    )(hidden_pre, grad_out, w_down.T)
    return grad_pre, grad_down.T


def solution(mesh):
    placed = (P("dp", "mp"), P("dp", None), P("mp", "dp"))
    return jax.shard_map(
        local, mesh=mesh, in_specs=placed, out_specs=(P("dp", "mp"), P("mp", "dp")), check_vma=False
    )
```

```python
import functools

import jax
import jax.numpy as jnp
from jax import lax
from jax.experimental import pallas as pl
from jax.experimental.pallas import tpu as pltpu
from jax.sharding import PartitionSpec as P

root_half = 0.7071067811865476
inv_root_tau = 0.3989422804014327

f32, bf16 = jnp.float32, jnp.bfloat16
MESH = pl.DeviceIdType.MESH

NX, NZL, NY, NZH = 4, 3, 8, 4
D, FF, TOKENS = 14848, 30720, 512
WIDE = 232
HALF = 1280
CHUNK = 256
NK = HALF // CHUNK
DZ = (0, 1, 3, 2, 2)
PIECE = (slice(0, HALF),) * 3 + (slice(0, HALF // 2), slice(HALF // 2, HALF))


def gelu_value(value):
    return 0.5 * value * (1.0 + lax.erf(value * root_half))


def gelu_slope(value):
    return (
        0.5 * (1.0 + lax.erf(value * root_half))
        + value * jnp.exp(-0.5 * value * value) * inv_root_tau
    )


def kernel(
    h_hbm, g_hbm, w_ref, gp_ref, gd_ref,
    h_ref, g_ref, slope, act_f, act_in, pf, pf_in, q, qin, gf, gt, a_all, w_own, w_in, wp,
    dyp, sb, rb, zs, z1, z2, z1_in, z2_in, fin, fin_in, raw, raw_in, gdv, ar_src, ar_in,
    local_sem, pair_s, pair_r, raw_s, raw_r, gy_s, gy_r, gz_s, gz_r, gx_s, gx_r,
    gd_s, gd_r, ay_s, ay_r, az_s, az_r, rs_s, rs_r, rz_s, rz_r, fin_s, fin_r, ar_s, ar_r,
):
    mp, dp = lax.axis_index("mp"), lax.axis_index("dp")
    x, zl = mp % NX, mp // NX
    c, y, zh = dp % 2, (dp // 2) % NY, dp // (2 * NY)
    oc = 1 - c

    def at(x_=None, zl_=None, c_=None, y_=None, zh_=None):
        x_ = x if x_ is None else x_
        zl_ = zl if zl_ is None else zl_
        c_ = c if c_ is None else c_
        y_ = y if y_ is None else y_
        zh_ = zh if zh_ is None else zh_
        return (zl_ * NX + x_, (zh_ * NY + y_) * 2 + c_)

    pair = at(c_=oc)
    later = []

    def copy(src, dst, ss, rs, to):
        return pltpu.make_async_remote_copy(
            src_ref=src, dst_ref=dst, send_sem=ss, recv_sem=rs, device_id=to, device_id_type=MESH
        )

    def send(src, dst, ss, rs, to):
        cp = copy(src, dst, ss, rs, to)
        cp.start()
        later.append(cp)

    def arrived(dst, ss, rs):
        copy(dst, dst, ss, rs, pair).wait_recv()

    g_copy = pltpu.make_async_copy(g_hbm, g_ref, local_sem.at[3])
    h_copy = pltpu.make_async_copy(h_hbm, h_ref, local_sem.at[4])
    g_copy.start()
    h_copy.start()
    barrier = pltpu.get_barrier_semaphore()
    depth = NZL * NZH
    along_z = [(NZL * zh + zl + r) % depth for r in range(1, depth)]
    along_z = [at(zl_=p % NZL, zh_=p // NZL) for p in along_z]
    along_y = [at(y_=(y + r) % NY) for r in range(1, NY)]
    along_x = [at(x_=(x + r) % NX) for r in range(1, NX)]
    across_x = [at(x_=(x + r) % NX, c_=oc) for r in range(1, NX)]
    peers = [along_z[r - 1] for r in (6, 5, 7, 4, 8, 3, 9)]
    peers += [along_y[r - 1] for r in (4, 3, 5, 2, 6)]
    peers += [along_z[r - 1] for r in (2, 10)] + [along_x[1]]
    peers += [along_y[0], along_y[6], along_x[0], along_x[2], along_z[0], along_z[10], pair]
    peers += across_x
    for peer in peers:
        pl.semaphore_signal(barrier, inc=1, device_id=peer, device_id_type=MESH)

    own_cols = pl.ds(pl.multiple_of(HALF * c, 128), HALF)
    other_cols = pl.ds(pl.multiple_of(HALF * oc, 128), HALF)
    w_copy = pltpu.make_async_copy(w_ref.at[:, own_cols], w_own, local_sem.at[0])
    w_copy.start()

    g_copy.wait()

    tile = x % 2
    first = WIDE * (x // 2) + 128 * tile
    lanes = lax.broadcasted_iota(jnp.int32, (8, 128), 1)
    keep = lanes < 128 - (256 - WIDE) * tile
    for d in range(NZH * NY):
        if d < NZH * NY - 1:
            off = 2 * WIDE * d + first
            start, width = (off // 128) * 128, 256
            window = g_ref[:, pl.ds(pl.multiple_of(start, 128), width)]
        else:
            off = 2 * WIDE * d + first
            start, width = D - 512, 512
            window = g_ref[:, start:start + width]
        rolled = pltpu.roll(window.astype(f32), width - (off - start), axis=1)
        pf[d] = jnp.where(keep, rolled[:, :128], 0.0)

    h_copy.wait()
    for half in range(2):
        hidden = h_ref[:, HALF * half:HALF * (half + 1)].astype(f32)
        act_f[half] = gelu_value(hidden).astype(bf16).astype(f32)

    pl.semaphore_wait(barrier, len(peers))
    send(pf.at[pl.ds(16 * oc, 16)], pf_in, pair_s.at[1], pair_r.at[1], pair)
    send(act_f.at[oc], act_in, pair_s.at[0], pair_r.at[0], pair)

    def rows_of(ys, zs_):
        return pl.ds(pl.multiple_of(64 * ys + 16 * zs_, 16), 16)

    def zj(j):
        return (zh + DZ[j]) % NZH

    def ys_of(way, t):
        return (y - t) % NY if way == 0 else (y + t) % NY

    def next_y(way):
        return at(y_=(y + 1) % NY) if way == 0 else at(y_=(y + NY - 1) % NY)

    def ways(t, j):
        if t < 3:
            return (0, 1)
        return (0,) if j < 2 else (1,)

    def piece(ys, j):
        return a_all.at[rows_of(ys, zj(j)), PIECE[j]]

    def gather(t, j):
        if t == 0 and j > 2:
            arrived(piece(y, j), az_s.at[j], az_r.at[j])
        for way in ways(t, j):
            block = piece(ys_of(way, t), j)
            if t > 0:
                arrived(block, ay_s.at[way, t - 1, j], ay_r.at[way, t - 1, j])
            send(block, block, ay_s.at[way, t, j], ay_r.at[way, t, j], next_y(way))

    up, down = at(zh_=(zh + 1) % NZH), at(zh_=(zh + NZH - 1) % NZH)

    def relay(i):
        j, to, half = ((2, up, 3), (1, down, 4))[i]
        arrived(piece(y, j), az_s.at[j], az_r.at[j])
        block = a_all.at[rows_of(y, zj(j)), PIECE[half]]
        send(block, block, az_s.at[half], az_r.at[half], to)

    arrived(pf_in, pair_s.at[1], pair_r.at[1])
    for j in range(2):
        for yd in range(NY):
            mine, theirs = pf[16 * c + 8 * j + yd], pf_in[8 * j + yd]
            q[j, yd] = jnp.concatenate(
                [jnp.where(c == 0, mine, theirs), jnp.where(c == 0, theirs, mine)], axis=0
            ).astype(bf16)
    for r in range(1, NY):
        to = (y + r) % NY
        send(q.at[:, to], qin.at[:, y], gy_s.at[r], gy_r.at[r], at(y_=to))
    qin[:, pl.ds(y, 1)] = q[:, pl.ds(y, 1)]

    arrived(act_in, pair_s.at[0], pair_r.at[0])
    mine, theirs = act_f[c], act_in[...]
    a_all[rows_of(y, zh), :] = jnp.concatenate(
        [jnp.where(c == 0, mine, theirs), jnp.where(c == 0, theirs, mine)], axis=0
    ).astype(bf16)
    own_block = a_all.at[rows_of(y, zh)]
    send(own_block, own_block, az_s.at[2], az_r.at[2], up)
    send(own_block, own_block, az_s.at[1], az_r.at[1], down)
    gather(0, 0)

    z16 = pl.ds(pl.multiple_of(16 * zh, 16), 16)
    holder = c == zh // 2

    def token_rows(dz):
        return pl.ds(pl.multiple_of(16 * ((zh + dz) % NZH), 16), 16)

    near, far = 2 * c + 1 - zh % 2, 2 * c + zh % 2
    near_at, far_at = at(zh_=near), at(zh_=far, zl_=(zl + 1) % NZL)

    def features_z():
        for r in range(1, NY):
            arrived(qin.at[:, (y + NY - r) % NY], gy_s.at[r], gy_r.at[r])
        send(qin.at[1 - zh % 2], gf.at[x, :, z16], gz_s.at[0], gz_r.at[zh], near_at)

        @pl.when(jnp.logical_not(holder))
        def _():
            copy(qin.at[zh % 2], gf.at[x, :, z16], gz_s.at[1], gz_r.at[zh], far_at).start()

        @pl.when(holder)
        def _():
            gf[x, :, z16, :] = qin[zh % 2]

    def features_x(dz):
        @pl.when(holder)
        def _():
            block = gf.at[x, :, token_rows(dz)]
            if dz > 0:
                copy(block, block, gz_s.at[0], gz_r.at[(zh + dz) % NZH], pair).wait_recv()
            for r in range(1, NX):
                copy(block, block, gx_s.at[r, dz], gx_r.at[r, dz], at(x_=(x + r) % NX)).start()
            copy(block, block, gd_s.at[0, dz], gd_r.at[0, dz], pair).start()

    def features_pair(dz):
        @pl.when(holder)
        def _():
            for r in range(1, NX):
                block = gf.at[(x + NX - r) % NX, :, token_rows(dz)]
                copy(block, block, gx_s.at[r, dz], gx_r.at[r, dz], pair).wait_recv()
                copy(block, block, gd_s.at[r, dz], gd_r.at[r, dz], pair).start()

    def features_here():
        @pl.when(jnp.logical_not(holder))
        def _():
            for dz in range(NZH):
                for r in range(NX):
                    block = gf.at[(x + NX - r) % NX, :, token_rows(dz)]
                    copy(block, block, gd_s.at[r, dz], gd_r.at[r, dz], pair).wait_recv()

    def weights():
        w_copy.wait()
        arrived(w_in, pair_s.at[2], pair_r.at[2])
        for b in range(2):
            wp[256 * b:256 * b + WIDE, :] = jnp.where(c == b, w_own[...], w_in[...])
            wp[256 * b + WIDE:256 * (b + 1), :] = jnp.zeros((256 - WIDE, HALF), bf16)

    def features():
        return jnp.concatenate([gf[i].reshape(TOKENS, 128) for i in range(NX)], axis=1)

    def turned():
        for i in range(NX):
            gt[128 * i:128 * (i + 1), :] = gf[i].reshape(TOKENS, 128).astype(f32).T.astype(bf16)

    def columns(k):
        return slice(CHUNK * k, CHUNK * (k + 1))

    def partial(yd, k, low, count):
        rows = pl.ds(pl.multiple_of(64 * yd + low, 16), count)
        return dyp[rows, columns(k)]

    def reduce_step(t, k):
        for way in range(2):
            if t == 0:
                part = (slice(0, 32),)
                val = partial((y + 4) % NY, k, 32 * way, 32)
            else:
                part = ()
                yd = (y + 4 - t) % NY if way == 0 else (y + NY - 4 + t) % NY
                if t == 1:
                    inc = rb.at[way, 0, k, slice(0, 32)]
                    arrived(inc, rs_s.at[way, 0, k], rs_r.at[way, 0, k])
                    low, high = partial(yd, k, 0, 32), partial(yd, k, 32, 32)
                    if way == 0:
                        low = low + inc[...].astype(f32)
                    else:
                        high = high + inc[...].astype(f32)
                    val = jnp.concatenate([low, high], axis=0)
                else:
                    inc = rb.at[way, t - 1, k]
                    arrived(inc, rs_s.at[way, t - 1, k], rs_r.at[way, t - 1, k])
                    val = partial(yd, k, 0, 64) + inc[...].astype(f32)
            src, dst = sb.at[(way, t, k) + part], rb.at[(way, t, k) + part]
            src[...] = val.astype(bf16)
            send(src, dst, rs_s.at[way, t, k], rs_r.at[way, t, k], next_y(way))

    def z_rows(dz):
        return pl.ds(pl.multiple_of(16 * ((zh + dz) % NZH), 16), 16)

    def reduce_z(k):
        val = partial(y, k, 0, 64)
        for way in range(2):
            inc = rb.at[way, 3, k]
            arrived(inc, rs_s.at[way, 3, k], rs_r.at[way, 3, k])
            val = val + inc[...].astype(f32)
        zs[k] = val
        for way, to in ((0, up), (1, down)):
            z1[k, way] = zs[k, z_rows(2), 128 * way:128 * (way + 1)]
            send(z1.at[k, way], z1_in.at[k, way], rz_s.at[k, way], rz_r.at[k, way], to)

    def reduce_z2(k):
        for way, to in ((0, up), (1, down)):
            arrived(z1_in.at[k, way], rz_s.at[k, way], rz_r.at[k, way])
            val = zs[k, z_rows(1 if way == 0 else 3), :]
            inc = z1_in[k, way]
            parts = [val[:, :128], val[:, 128:]]
            parts[way] = parts[way] + inc
            z2[k, way] = jnp.concatenate(parts, axis=1)
            send(z2.at[k, way], z2_in.at[k, way], rz_s.at[k, 2 + way], rz_r.at[k, 2 + way], to)

    def reduce_end(k):
        val = zs[k, z_rows(0), :]
        for way in range(2):
            arrived(z2_in.at[k, way], rz_s.at[k, 2 + way], rz_r.at[k, 2 + way])
            val = val + z2_in[k, way]
        fin[k, 0] = val[0:8]
        fin[k, 1] = val[8:16]
        send(fin.at[k, oc], fin_in.at[k], fin_s.at[k], fin_r.at[k], pair)

    def product(k):
        dyp[:, columns(k)] = lax.dot_general(
            features(), wp[:, columns(k)], (((1,), (0,)), ((), ())), preferred_element_type=f32
        )

    def gathered():
        for j in range(len(DZ)):
            for way in range(2):
                t = 3 if way in ways(3, j) else 2
                arrived(piece(ys_of(way, t + 1), j), ay_s.at[way, t, j], ay_r.at[way, t, j])

    def weight_grad(k):
        val = lax.dot_general(
            gt[...], a_all[:, columns(k)], (((1,), (0,)), ((), ())), preferred_element_type=f32
        )
        for b in range(2):
            raw[b, :, columns(k)] = val[256 * b:256 * b + WIDE]
        send(
            raw.at[oc, :, columns(k)], raw_in.at[:, columns(k)], raw_s.at[k], raw_r.at[k], pair
        )
        part = jnp.sum((val * val).reshape(512 // 8, 8, CHUNK), axis=0)
        part = part[:, 0:128] + part[:, 128:256]
        ar_src[0] = part if k == 0 else ar_src[0] + part

    stages = (
        [pair] + along_x + across_x,
        [at(y_=(y + r) % NY) for r in range(1, NY)],
        along_z,
    )
    begin = [sum(len(s) for s in stages[:i]) for i in range(len(stages) + 1)]

    def sum_send(i):
        for n, to in enumerate(stages[i]):
            slot = begin[i] + n
            send(ar_src.at[i], ar_in.at[slot], ar_s.at[slot], ar_r.at[slot], to)

    def sum_wait(i):
        val = ar_src[i]
        for slot in range(begin[i], begin[i + 1]):
            arrived(ar_in.at[slot], ar_s.at[slot], ar_r.at[slot])
            val = val + ar_in[slot]
        ar_src[i + 1] = val

    def scaled():
        sumsq = jnp.sum(ar_src[3])
        rms = jnp.sqrt(jnp.full((8, 128), sumsq, f32) / (float(FF) * float(D)) + 1e-06)
        scale = jnp.minimum(1.0, 1.0 / rms)[0:1, 0:1]
        gdv[:, own_cols] = (raw[c] * scale).astype(bf16)
        out0 = pltpu.make_async_copy(gdv.at[:, own_cols], gd_ref.at[:, own_cols], local_sem.at[1])
        out0.start()
        for k in range(NK):
            arrived(raw_in.at[:, columns(k)], raw_s.at[k], raw_r.at[k])
        gdv[:, other_cols] = (raw_in[...] * scale).astype(bf16)
        out1 = pltpu.make_async_copy(
            gdv.at[:, other_cols], gd_ref.at[:, other_cols], local_sem.at[2]
        )
        out1.start()
        return out0, out1

    def slopes():
        for half in range(2):
            slope[half] = gelu_slope(h_ref[:, HALF * half:HALF * (half + 1)].astype(f32))

    send(w_ref.at[:, other_cols], w_in, pair_s.at[2], pair_r.at[2], pair)
    slopes()
    weights()
    gather(1, 0)
    features_z()
    features_x(0)
    relay(0)
    relay(1)
    gather(0, 2)
    gather(0, 1)
    gather(2, 0)
    gather(1, 2)
    features_pair(0)
    features_x(1)
    features_x(3)
    gather(1, 1)
    gather(3, 0)
    gather(0, 3)
    features_x(2)
    gather(0, 4)
    gather(2, 2)
    gather(2, 1)
    features_pair(1)
    gather(1, 3)
    features_pair(3)
    gather(1, 4)
    features_pair(2)
    gather(3, 2)
    gather(3, 1)
    features_here()
    gather(2, 3)
    gather(2, 4)
    product(0)
    reduce_step(0, 0)
    product(1)
    reduce_step(0, 1)
    product(2)
    reduce_step(0, 2)
    product(3)
    reduce_step(0, 3)
    product(4)
    reduce_step(0, 4)
    gather(3, 3)
    gather(3, 4)
    reduce_step(1, 0)
    reduce_step(1, 1)
    reduce_step(1, 2)
    reduce_step(1, 3)
    reduce_step(1, 4)
    turned()
    gathered()
    weight_grad(0)
    weight_grad(1)
    reduce_step(2, 0)
    weight_grad(2)
    weight_grad(3)
    weight_grad(4)
    sum_send(0)
    reduce_step(2, 1)
    reduce_step(2, 2)
    reduce_step(2, 3)
    reduce_step(2, 4)
    reduce_step(3, 0)
    reduce_step(3, 1)
    reduce_step(3, 2)
    sum_wait(0)
    sum_send(1)
    reduce_step(3, 3)
    reduce_step(3, 4)
    reduce_z(0)
    reduce_z(1)
    reduce_z(2)
    reduce_z(3)
    reduce_z(4)
    reduce_z2(0)
    reduce_z2(1)
    sum_wait(1)
    sum_send(2)
    reduce_z2(2)
    reduce_z2(3)
    reduce_z2(4)
    reduce_end(0)
    reduce_end(1)
    reduce_end(2)
    reduce_end(3)
    reduce_end(4)
    sum_wait(2)
    outs = scaled()

    for k in range(NK):
        arrived(fin_in.at[k], fin_s.at[k], fin_r.at[k])
        mine, theirs = fin[k, c], fin_in[k]
        for half in range(2):
            cols = slice(HALF * half + CHUNK * k, HALF * half + CHUNK * (k + 1))
            gp_ref[:, cols] = (jnp.where(c == half, mine, theirs) * slope[half, :, columns(k)]).astype(bf16)

    for cp in later:
        cp.wait_send()
    @pl.when(jnp.logical_not(holder))
    def _():
        copy(qin.at[0], gf.at[x, :, z16], gz_s.at[1], gz_r.at[zh], pair).wait_send()

    @pl.when(holder)
    def _():
        for dz in range(NZH):
            block = gf.at[x, :, token_rows(dz)]
            for r in range(NX):
                if r > 0:
                    copy(block, block, gx_s.at[r, dz], gx_r.at[r, dz], pair).wait_send()
                copy(block, block, gd_s.at[r, dz], gd_r.at[r, dz], pair).wait_send()

    for out in outs:
        out.wait()


def local(hidden_pre, grad_out, w_down):
    dma = pltpu.SemaphoreType.DMA
    vmem = pltpu.VMEM
    n_sum = 2 * NX - 1 + (NY - 1) + (NZL * NZH - 1)
    sems = [
        (5,), (3,), (3,), (NK,), (NK,), (NY,), (NY,), (2,), (NZH,), (NX, NZH), (NX, NZH),
        (NX, NZH), (NX, NZH), (2, 4, 5), (2, 4, 5), (5,), (5,), (2, 4, NK), (2, 4, NK),
        (NK, 4), (NK, 4), (NK,), (NK,), (n_sum,), (n_sum,),
    ]
    grad_pre, grad_down = pl.pallas_call(
        kernel,
        out_shape=(
            jax.ShapeDtypeStruct(hidden_pre.shape, bf16),
            jax.ShapeDtypeStruct(w_down.T.shape, bf16),
        ),
        in_specs=[
            pl.BlockSpec(memory_space=pl.ANY),
            pl.BlockSpec(memory_space=pl.ANY),
            pl.BlockSpec(memory_space=pl.ANY),
        ],
        out_specs=(
            pl.BlockSpec(memory_space=pltpu.VMEM),
            pl.BlockSpec(memory_space=pl.ANY),
        ),
        scratch_shapes=[
            vmem((8, 2 * HALF), bf16),
            vmem((8, D), bf16),
            vmem((2, 8, HALF), f32),
            vmem((2, 8, HALF), f32),
            vmem((8, HALF), f32),
            vmem((NZH * NY, 8, 128), f32),
            vmem((16, 8, 128), f32),
            vmem((2, NY, 16, 128), bf16),
            vmem((2, NY, 16, 128), bf16),
            vmem((NX, NY, 64, 128), bf16),
            vmem((512, TOKENS), bf16),
            vmem((TOKENS, HALF), bf16),
            vmem((WIDE, HALF), bf16),
            vmem((WIDE, HALF), bf16),
            vmem((512, HALF), bf16),
            vmem((TOKENS, HALF), f32),
            vmem((2, 4, NK, 64, CHUNK), bf16),
            vmem((2, 4, NK, 64, CHUNK), bf16),
            vmem((NK, 64, CHUNK), f32),
            vmem((NK, 2, 16, 128), f32),
            vmem((NK, 2, 16, CHUNK), f32),
            vmem((NK, 2, 16, 128), f32),
            vmem((NK, 2, 16, CHUNK), f32),
            vmem((NK, 2, 8, CHUNK), f32),
            vmem((NK, 8, CHUNK), f32),
            vmem((2, WIDE, HALF), f32),
            vmem((WIDE, HALF), f32),
            vmem((WIDE, 2 * HALF), bf16),
            vmem((5, 8, 128), f32),
            vmem((n_sum, 8, 128), f32),
        ] + [dma(s) for s in sems],
        compiler_params=pltpu.CompilerParams(
            collective_id=0, has_side_effects=True, vmem_limit_bytes=53632 * 1024
        ),
        cost_estimate=pl.CostEstimate(
            flops=4 * TOKENS * 2 * HALF * WIDE, bytes_accessed=6 << 20, transcendentals=0
        ),
    )(hidden_pre, grad_out, w_down.T)
    return grad_pre, grad_down.T


def solution(mesh):
    placed = (P("dp", "mp"), P("dp", None), P("mp", "dp"))
    return jax.shard_map(
        local, mesh=mesh, in_specs=placed, out_specs=(P("dp", "mp"), P("mp", "dp")), check_vma=False
    )
```

```python
import functools

import jax
import jax.numpy as jnp
from jax import lax
from jax.experimental import pallas as pl
from jax.experimental.pallas import tpu as pltpu
from jax.sharding import PartitionSpec as P

root_half = 0.7071067811865476
inv_root_tau = 0.3989422804014327

f32, bf16 = jnp.float32, jnp.bfloat16
MESH = pl.DeviceIdType.MESH

NX, NZL, NY, NZH = 4, 3, 8, 4
D, FF, TOKENS = 14848, 30720, 512
WIDE = 232
HALF = 1280
CHUNK = 256
NK = HALF // CHUNK
DZ = (0, 1, 3, 2, 2)
PIECE = (slice(0, HALF),) * 3 + (slice(0, HALF // 2), slice(HALF // 2, HALF))


def gelu_value(value):
    return 0.5 * value * (1.0 + lax.erf(value * root_half))


def gelu_slope(value):
    return (
        0.5 * (1.0 + lax.erf(value * root_half))
        + value * jnp.exp(-0.5 * value * value) * inv_root_tau
    )


def kernel(
    h_hbm, g_hbm, w_ref, gp_ref, gd_ref,
    h_ref, g_ref, slope, act_f, act_in, pf, pf_in, q, qin, gf, gt, a_all, w_own, w_in, wp,
    dyp, sb, rb, zs, z1, z2, z1_in, z2_in, fin, fin_in, raw, raw_in, gdv, ar_src, ar_in,
    local_sem, pair_s, pair_r, raw_s, raw_r, gy_s, gy_r, gz_s, gz_r, gx_s, gx_r,
    gd_s, gd_r, ay_s, ay_r, az_s, az_r, rs_s, rs_r, rz_s, rz_r, fin_s, fin_r, ar_s, ar_r,
):
    mp, dp = lax.axis_index("mp"), lax.axis_index("dp")
    x, zl = mp % NX, mp // NX
    c, y, zh = dp % 2, (dp // 2) % NY, dp // (2 * NY)
    oc = 1 - c

    def at(x_=None, zl_=None, c_=None, y_=None, zh_=None):
        x_ = x if x_ is None else x_
        zl_ = zl if zl_ is None else zl_
        c_ = c if c_ is None else c_
        y_ = y if y_ is None else y_
        zh_ = zh if zh_ is None else zh_
        return (zl_ * NX + x_, (zh_ * NY + y_) * 2 + c_)

    pair = at(c_=oc)
    later = []

    def copy(src, dst, ss, rs, to):
        return pltpu.make_async_remote_copy(
            src_ref=src, dst_ref=dst, send_sem=ss, recv_sem=rs, device_id=to, device_id_type=MESH
        )

    def send(src, dst, ss, rs, to):
        cp = copy(src, dst, ss, rs, to)
        cp.start()
        later.append(cp)

    def arrived(dst, ss, rs):
        copy(dst, dst, ss, rs, pair).wait_recv()

    g_copy = pltpu.make_async_copy(g_hbm, g_ref, local_sem.at[3])
    h_copy = pltpu.make_async_copy(h_hbm, h_ref, local_sem.at[4])
    g_copy.start()
    h_copy.start()
    barrier = pltpu.get_barrier_semaphore()
    depth = NZL * NZH
    along_z = [(NZL * zh + zl + r) % depth for r in range(1, depth)]
    along_z = [at(zl_=p % NZL, zh_=p // NZL) for p in along_z]
    along_y = [at(y_=(y + r) % NY) for r in range(1, NY)]
    along_x = [at(x_=(x + r) % NX) for r in range(1, NX)]
    across_x = [at(x_=(x + r) % NX, c_=oc) for r in range(1, NX)]
    peers = [along_z[r - 1] for r in (6, 5, 7, 4, 8, 3, 9)]
    peers += [along_y[r - 1] for r in (4, 3, 5, 2, 6)]
    peers += [along_z[r - 1] for r in (2, 10)] + [along_x[1]]
    peers += [along_y[0], along_y[6], along_x[0], along_x[2], along_z[0], along_z[10], pair]
    peers += across_x
    for peer in peers:
        pl.semaphore_signal(barrier, inc=1, device_id=peer, device_id_type=MESH)

    own_cols = pl.ds(pl.multiple_of(HALF * c, 128), HALF)
    other_cols = pl.ds(pl.multiple_of(HALF * oc, 128), HALF)
    w_copy = pltpu.make_async_copy(w_ref.at[:, own_cols], w_own, local_sem.at[0])
    w_copy.start()

    g_copy.wait()

    tile = x % 2
    first = WIDE * (x // 2) + 128 * tile
    lanes = lax.broadcasted_iota(jnp.int32, (8, 128), 1)
    keep = lanes < 128 - (256 - WIDE) * tile
    for d in range(NZH * NY):
        if d < NZH * NY - 1:
            off = 2 * WIDE * d + first
            start, width = (off // 128) * 128, 256
            window = g_ref[:, pl.ds(pl.multiple_of(start, 128), width)]
        else:
            off = 2 * WIDE * d + first
            start, width = D - 512, 512
            window = g_ref[:, start:start + width]
        rolled = pltpu.roll(window.astype(f32), width - (off - start), axis=1)
        pf[d] = jnp.where(keep, rolled[:, :128], 0.0)

    h_copy.wait()
    for half in range(2):
        hidden = h_ref[:, HALF * half:HALF * (half + 1)].astype(f32)
        act_f[half] = gelu_value(hidden).astype(bf16).astype(f32)

    pl.semaphore_wait(barrier, len(peers))
    send(pf.at[pl.ds(16 * oc, 16)], pf_in, pair_s.at[1], pair_r.at[1], pair)
    send(act_f.at[oc], act_in, pair_s.at[0], pair_r.at[0], pair)

    def rows_of(ys, zs_):
        return pl.ds(pl.multiple_of(64 * ys + 16 * zs_, 16), 16)

    def zj(j):
        return (zh + DZ[j]) % NZH

    def ys_of(way, t):
        return (y - t) % NY if way == 0 else (y + t) % NY

    def next_y(way):
        return at(y_=(y + 1) % NY) if way == 0 else at(y_=(y + NY - 1) % NY)

    def ways(t, j):
        if t < 3:
            return (0, 1)
        return (0,) if j < 2 else (1,)

    def piece(ys, j):
        return a_all.at[rows_of(ys, zj(j)), PIECE[j]]

    def gather(t, j):
        if t == 0 and j > 2:
            arrived(piece(y, j), az_s.at[j], az_r.at[j])
        for way in ways(t, j):
            block = piece(ys_of(way, t), j)
            if t > 0:
                arrived(block, ay_s.at[way, t - 1, j], ay_r.at[way, t - 1, j])
            send(block, block, ay_s.at[way, t, j], ay_r.at[way, t, j], next_y(way))

    up, down = at(zh_=(zh + 1) % NZH), at(zh_=(zh + NZH - 1) % NZH)

    def relay(i):
        j, to, half = ((2, up, 3), (1, down, 4))[i]
        arrived(piece(y, j), az_s.at[j], az_r.at[j])
        block = a_all.at[rows_of(y, zj(j)), PIECE[half]]
        send(block, block, az_s.at[half], az_r.at[half], to)

    arrived(pf_in, pair_s.at[1], pair_r.at[1])
    for j in range(2):
        for yd in range(NY):
            mine, theirs = pf[16 * c + 8 * j + yd], pf_in[8 * j + yd]
            q[j, yd] = jnp.concatenate(
                [jnp.where(c == 0, mine, theirs), jnp.where(c == 0, theirs, mine)], axis=0
            ).astype(bf16)
    for r in range(1, NY):
        to = (y + r) % NY
        send(q.at[:, to], qin.at[:, y], gy_s.at[r], gy_r.at[r], at(y_=to))
    qin[:, pl.ds(y, 1)] = q[:, pl.ds(y, 1)]

    arrived(act_in, pair_s.at[0], pair_r.at[0])
    mine, theirs = act_f[c], act_in[...]
    a_all[rows_of(y, zh), :] = jnp.concatenate(
        [jnp.where(c == 0, mine, theirs), jnp.where(c == 0, theirs, mine)], axis=0
    ).astype(bf16)
    own_block = a_all.at[rows_of(y, zh)]
    send(own_block, own_block, az_s.at[2], az_r.at[2], up)
    send(own_block, own_block, az_s.at[1], az_r.at[1], down)
    gather(0, 0)

    z16 = pl.ds(pl.multiple_of(16 * zh, 16), 16)
    holder = c == zh // 2

    def token_rows(dz):
        return pl.ds(pl.multiple_of(16 * ((zh + dz) % NZH), 16), 16)

    near, far = 2 * c + 1 - zh % 2, 2 * c + zh % 2
    near_at, far_at = at(zh_=near), at(zh_=far, zl_=(zl + 1) % NZL)

    def features_z():
        for r in range(1, NY):
            arrived(qin.at[:, (y + NY - r) % NY], gy_s.at[r], gy_r.at[r])
        send(qin.at[1 - zh % 2], gf.at[x, :, z16], gz_s.at[0], gz_r.at[zh], near_at)

        @pl.when(jnp.logical_not(holder))
        def _():
            copy(qin.at[zh % 2], gf.at[x, :, z16], gz_s.at[1], gz_r.at[zh], far_at).start()

        @pl.when(holder)
        def _():
            gf[x, :, z16, :] = qin[zh % 2]

    def features_x(dz):
        @pl.when(holder)
        def _():
            block = gf.at[x, :, token_rows(dz)]
            if dz > 0:
                copy(block, block, gz_s.at[0], gz_r.at[(zh + dz) % NZH], pair).wait_recv()
            for r in range(1, NX):
                copy(block, block, gx_s.at[r, dz], gx_r.at[r, dz], at(x_=(x + r) % NX)).start()
            copy(block, block, gd_s.at[0, dz], gd_r.at[0, dz], pair).start()

    def features_pair(dz):
        @pl.when(holder)
        def _():
            for r in range(1, NX):
                block = gf.at[(x + NX - r) % NX, :, token_rows(dz)]
                copy(block, block, gx_s.at[r, dz], gx_r.at[r, dz], pair).wait_recv()
                copy(block, block, gd_s.at[r, dz], gd_r.at[r, dz], pair).start()

    def features_here():
        @pl.when(jnp.logical_not(holder))
        def _():
            for dz in range(NZH):
                for r in range(NX):
                    block = gf.at[(x + NX - r) % NX, :, token_rows(dz)]
                    copy(block, block, gd_s.at[r, dz], gd_r.at[r, dz], pair).wait_recv()

    def weights():
        w_copy.wait()
        arrived(w_in, pair_s.at[2], pair_r.at[2])
        for b in range(2):
            wp[256 * b:256 * b + WIDE, :] = jnp.where(c == b, w_own[...], w_in[...])
            wp[256 * b + WIDE:256 * (b + 1), :] = jnp.zeros((256 - WIDE, HALF), bf16)

    def features():
        return jnp.concatenate([gf[i].reshape(TOKENS, 128) for i in range(NX)], axis=1)

    def turned():
        for i in range(NX):
            gt[128 * i:128 * (i + 1), :] = gf[i].reshape(TOKENS, 128).astype(f32).T.astype(bf16)

    def columns(k):
        return slice(CHUNK * k, CHUNK * (k + 1))

    def partial(yd, k, low, count):
        rows = pl.ds(pl.multiple_of(64 * yd + low, 16), count)
        return dyp[rows, columns(k)]

    def reduce_step(t, k):
        for way in range(2):
            if t == 0:
                part = (slice(0, 32),)
                val = partial((y + 4) % NY, k, 32 * way, 32)
            else:
                part = ()
                yd = (y + 4 - t) % NY if way == 0 else (y + NY - 4 + t) % NY
                if t == 1:
                    inc = rb.at[way, 0, k, slice(0, 32)]
                    arrived(inc, rs_s.at[way, 0, k], rs_r.at[way, 0, k])
                    low, high = partial(yd, k, 0, 32), partial(yd, k, 32, 32)
                    if way == 0:
                        low = low + inc[...].astype(f32)
                    else:
                        high = high + inc[...].astype(f32)
                    val = jnp.concatenate([low, high], axis=0)
                else:
                    inc = rb.at[way, t - 1, k]
                    arrived(inc, rs_s.at[way, t - 1, k], rs_r.at[way, t - 1, k])
                    val = partial(yd, k, 0, 64) + inc[...].astype(f32)
            src, dst = sb.at[(way, t, k) + part], rb.at[(way, t, k) + part]
            src[...] = val.astype(bf16)
            send(src, dst, rs_s.at[way, t, k], rs_r.at[way, t, k], next_y(way))

    def z_rows(dz):
        return pl.ds(pl.multiple_of(16 * ((zh + dz) % NZH), 16), 16)

    def reduce_z(k):
        val = partial(y, k, 0, 64)
        for way in range(2):
            inc = rb.at[way, 3, k]
            arrived(inc, rs_s.at[way, 3, k], rs_r.at[way, 3, k])
            val = val + inc[...].astype(f32)
        zs[k] = val
        for way, to in ((0, up), (1, down)):
            z1[k, way] = zs[k, z_rows(2), 128 * way:128 * (way + 1)]
            send(z1.at[k, way], z1_in.at[k, way], rz_s.at[k, way], rz_r.at[k, way], to)

    def reduce_z2(k):
        for way, to in ((0, up), (1, down)):
            arrived(z1_in.at[k, way], rz_s.at[k, way], rz_r.at[k, way])
            val = zs[k, z_rows(1 if way == 0 else 3), :]
            inc = z1_in[k, way]
            parts = [val[:, :128], val[:, 128:]]
            parts[way] = parts[way] + inc
            z2[k, way] = jnp.concatenate(parts, axis=1)
            send(z2.at[k, way], z2_in.at[k, way], rz_s.at[k, 2 + way], rz_r.at[k, 2 + way], to)

    def reduce_end(k):
        val = zs[k, z_rows(0), :]
        for way in range(2):
            arrived(z2_in.at[k, way], rz_s.at[k, 2 + way], rz_r.at[k, 2 + way])
            val = val + z2_in[k, way]
        fin[k, 0] = val[0:8]
        fin[k, 1] = val[8:16]
        send(fin.at[k, oc], fin_in.at[k], fin_s.at[k], fin_r.at[k], pair)

    def product(k):
        dyp[:, columns(k)] = lax.dot_general(
            features(), wp[:, columns(k)], (((1,), (0,)), ((), ())), preferred_element_type=f32
        )

    def gathered():
        for j in range(len(DZ)):
            for way in range(2):
                t = 3 if way in ways(3, j) else 2
                arrived(piece(ys_of(way, t + 1), j), ay_s.at[way, t, j], ay_r.at[way, t, j])

    def weight_grad(k):
        val = lax.dot_general(
            gt[...], a_all[:, columns(k)], (((1,), (0,)), ((), ())), preferred_element_type=f32
        )
        for b in range(2):
            raw[b, :, columns(k)] = val[256 * b:256 * b + WIDE]
        send(
            raw.at[oc, :, columns(k)], raw_in.at[:, columns(k)], raw_s.at[k], raw_r.at[k], pair
        )
        part = jnp.sum((val * val).reshape(512 // 8, 8, CHUNK), axis=0)
        part = part[:, 0:128] + part[:, 128:256]
        ar_src[0] = part if k == 0 else ar_src[0] + part

    stages = (
        [pair] + along_x + across_x,
        [at(y_=(y + r) % NY) for r in range(1, NY)],
        along_z,
    )
    begin = [sum(len(s) for s in stages[:i]) for i in range(len(stages) + 1)]

    def sum_send(i):
        for n, to in enumerate(stages[i]):
            slot = begin[i] + n
            send(ar_src.at[i], ar_in.at[slot], ar_s.at[slot], ar_r.at[slot], to)

    def sum_wait(i):
        val = ar_src[i]
        for slot in range(begin[i], begin[i + 1]):
            arrived(ar_in.at[slot], ar_s.at[slot], ar_r.at[slot])
            val = val + ar_in[slot]
        ar_src[i + 1] = val

    def scaled():
        sumsq = jnp.sum(ar_src[3])
        rms = jnp.sqrt(jnp.full((8, 128), sumsq, f32) / (float(FF) * float(D)) + 1e-06)
        scale = jnp.minimum(1.0, 1.0 / rms)[0:1, 0:1]
        gdv[:, own_cols] = (raw[c] * scale).astype(bf16)
        out0 = pltpu.make_async_copy(gdv.at[:, own_cols], gd_ref.at[:, own_cols], local_sem.at[1])
        out0.start()
        for k in range(NK):
            arrived(raw_in.at[:, columns(k)], raw_s.at[k], raw_r.at[k])
        gdv[:, other_cols] = (raw_in[...] * scale).astype(bf16)
        out1 = pltpu.make_async_copy(
            gdv.at[:, other_cols], gd_ref.at[:, other_cols], local_sem.at[2]
        )
        out1.start()
        return out0, out1

    def slopes():
        for half in range(2):
            slope[half] = gelu_slope(h_ref[:, HALF * half:HALF * (half + 1)].astype(f32))

    send(w_ref.at[:, other_cols], w_in, pair_s.at[2], pair_r.at[2], pair)
    gather(1, 0)
    features_z()
    features_x(0)
    relay(0)
    relay(1)
    gather(0, 2)
    gather(0, 1)
    gather(2, 0)
    gather(1, 2)
    features_pair(0)
    slopes()
    weights()
    features_x(1)
    features_x(3)
    gather(1, 1)
    gather(3, 0)
    gather(0, 3)
    features_x(2)
    gather(0, 4)
    gather(2, 2)
    gather(2, 1)
    features_pair(1)
    gather(1, 3)
    features_pair(3)
    gather(1, 4)
    features_pair(2)
    gather(3, 2)
    gather(3, 1)
    features_here()
    gather(2, 3)
    gather(2, 4)
    product(0)
    reduce_step(0, 0)
    product(1)
    reduce_step(0, 1)
    product(2)
    reduce_step(0, 2)
    product(3)
    reduce_step(0, 3)
    product(4)
    reduce_step(0, 4)
    gather(3, 3)
    gather(3, 4)
    reduce_step(1, 0)
    reduce_step(1, 1)
    reduce_step(1, 2)
    reduce_step(1, 3)
    reduce_step(1, 4)
    turned()
    gathered()
    weight_grad(0)
    weight_grad(1)
    reduce_step(2, 0)
    weight_grad(2)
    weight_grad(3)
    weight_grad(4)
    sum_send(0)
    reduce_step(2, 1)
    reduce_step(2, 2)
    reduce_step(2, 3)
    reduce_step(2, 4)
    reduce_step(3, 0)
    reduce_step(3, 1)
    reduce_step(3, 2)
    sum_wait(0)
    sum_send(1)
    reduce_step(3, 3)
    reduce_step(3, 4)
    reduce_z(0)
    reduce_z(1)
    reduce_z(2)
    reduce_z(3)
    reduce_z(4)
    reduce_z2(0)
    reduce_z2(1)
    sum_wait(1)
    sum_send(2)
    reduce_z2(2)
    reduce_z2(3)
    reduce_z2(4)
    reduce_end(0)
    reduce_end(1)
    reduce_end(2)
    reduce_end(3)
    reduce_end(4)
    sum_wait(2)
    outs = scaled()

    for k in range(NK):
        arrived(fin_in.at[k], fin_s.at[k], fin_r.at[k])
        mine, theirs = fin[k, c], fin_in[k]
        for half in range(2):
            cols = slice(HALF * half + CHUNK * k, HALF * half + CHUNK * (k + 1))
            gp_ref[:, cols] = (jnp.where(c == half, mine, theirs) * slope[half, :, columns(k)]).astype(bf16)

    for cp in later:
        cp.wait_send()
    @pl.when(jnp.logical_not(holder))
    def _():
        copy(qin.at[0], gf.at[x, :, z16], gz_s.at[1], gz_r.at[zh], pair).wait_send()

    @pl.when(holder)
    def _():
        for dz in range(NZH):
            block = gf.at[x, :, token_rows(dz)]
            for r in range(NX):
                if r > 0:
                    copy(block, block, gx_s.at[r, dz], gx_r.at[r, dz], pair).wait_send()
                copy(block, block, gd_s.at[r, dz], gd_r.at[r, dz], pair).wait_send()

    for out in outs:
        out.wait()


def local(hidden_pre, grad_out, w_down):
    dma = pltpu.SemaphoreType.DMA
    vmem = pltpu.VMEM
    n_sum = 2 * NX - 1 + (NY - 1) + (NZL * NZH - 1)
    sems = [
        (5,), (3,), (3,), (NK,), (NK,), (NY,), (NY,), (2,), (NZH,), (NX, NZH), (NX, NZH),
        (NX, NZH), (NX, NZH), (2, 4, 5), (2, 4, 5), (5,), (5,), (2, 4, NK), (2, 4, NK),
        (NK, 4), (NK, 4), (NK,), (NK,), (n_sum,), (n_sum,),
    ]
    grad_pre, grad_down = pl.pallas_call(
        kernel,
        out_shape=(
            jax.ShapeDtypeStruct(hidden_pre.shape, bf16),
            jax.ShapeDtypeStruct(w_down.T.shape, bf16),
        ),
        in_specs=[
            pl.BlockSpec(memory_space=pl.ANY),
            pl.BlockSpec(memory_space=pl.ANY),
            pl.BlockSpec(memory_space=pl.ANY),
        ],
        out_specs=(
            pl.BlockSpec(memory_space=pltpu.VMEM),
            pl.BlockSpec(memory_space=pl.ANY),
        ),
        scratch_shapes=[
            vmem((8, 2 * HALF), bf16),
            vmem((8, D), bf16),
            vmem((2, 8, HALF), f32),
            vmem((2, 8, HALF), f32),
            vmem((8, HALF), f32),
            vmem((NZH * NY, 8, 128), f32),
            vmem((16, 8, 128), f32),
            vmem((2, NY, 16, 128), bf16),
            vmem((2, NY, 16, 128), bf16),
            vmem((NX, NY, 64, 128), bf16),
            vmem((512, TOKENS), bf16),
            vmem((TOKENS, HALF), bf16),
            vmem((WIDE, HALF), bf16),
            vmem((WIDE, HALF), bf16),
            vmem((512, HALF), bf16),
            vmem((TOKENS, HALF), f32),
            vmem((2, 4, NK, 64, CHUNK), bf16),
            vmem((2, 4, NK, 64, CHUNK), bf16),
            vmem((NK, 64, CHUNK), f32),
            vmem((NK, 2, 16, 128), f32),
            vmem((NK, 2, 16, CHUNK), f32),
            vmem((NK, 2, 16, 128), f32),
            vmem((NK, 2, 16, CHUNK), f32),
            vmem((NK, 2, 8, CHUNK), f32),
            vmem((NK, 8, CHUNK), f32),
            vmem((2, WIDE, HALF), f32),
            vmem((WIDE, HALF), f32),
            vmem((WIDE, 2 * HALF), bf16),
            vmem((5, 8, 128), f32),
            vmem((n_sum, 8, 128), f32),
        ] + [dma(s) for s in sems],
        compiler_params=pltpu.CompilerParams(
            collective_id=0, has_side_effects=True, vmem_limit_bytes=53632 * 1024
        ),
        cost_estimate=pl.CostEstimate(
            flops=4 * TOKENS * 2 * HALF * WIDE, bytes_accessed=6 << 20, transcendentals=0
        ),
    )(hidden_pre, grad_out, w_down.T)
    return grad_pre, grad_down.T


def solution(mesh):
    placed = (P("dp", "mp"), P("dp", None), P("mp", "dp"))
    return jax.shard_map(
        local, mesh=mesh, in_specs=placed, out_specs=(P("dp", "mp"), P("mp", "dp")), check_vma=False
    )
```
